32 devices in a mesh: feat: 8 (over z, y), dp: 4 (over x, core).
Axes of the slice: x: 2, y: 2, z: 4, core: 2. Of those that a mesh axis runs over, the one named last changes fastest.
Arguments:
- query_grads: bfloat16 [64, 131072], P(('dp', 'feat')), may hold values from -52 to 52
- build_grads: bfloat16 [512, 131072], P('dp', 'feat'), may hold values from -52 to 52
- scored_grads: bfloat16 [2048, 131072], P('dp', 'feat'), may hold values from -52 to 52
Outputs:
- scores: float32 [2048, 64], P(('dp', 'feat'))
The draws below stay inside these ranges and needn't reach their ends.
All inputs are finite; a program needn't handle non-finite values.
Results may differ from the reference program's by a relative error of at most 0.0049.
Values may be sent and summed in bfloat16 or wider, within the bound.
A program may use at most 128 MiB of HBM per device.

```python
import math
import jax
import jax.numpy as jnp
from jax import lax

MATS = 32
FEAT = 131072
NQ = 64
NB = 512
NS = 2048


def feature_scale(base_key):
    spread = jax.random.uniform(jax.random.fold_in(base_key, 11), (FEAT,), jnp.float32)
    position = jnp.arange(FEAT, dtype=jnp.float32) / FEAT
    return jnp.exp(jnp.log(3.0) * position + jnp.log(3.3) * spread)


def shared_part(base_key, own_key, row_count):
    group_count = MATS * 2
    group_span = FEAT // group_count
    ranking = jax.random.permutation(jax.random.fold_in(base_key, 17), group_count)
    harmonic = math.log(group_count) + 0.5772 + 0.5 / group_count
    strength = jnp.sqrt(group_count / harmonic / (ranking.astype(jnp.float32) + 1.0))
    direction = jnp.clip(jax.random.normal(jax.random.fold_in(base_key, 19), (group_count, group_span), jnp.float32), -4.0, 4.0)
    loadings = jnp.clip(jax.random.normal(jax.random.fold_in(own_key, 3), (row_count, group_count), jnp.float32), -4.0, 4.0)
    blocks = (loadings * strength[None, :])[:, :, None] * direction[None, :, :]
    return blocks.reshape(row_count, FEAT)


def example_rows(base_key, salt_value, row_count):
    own_key = jax.random.fold_in(base_key, salt_value)
    spread = jax.random.uniform(jax.random.fold_in(own_key, 1), (row_count,), jnp.float32)
    position = jnp.arange(row_count, dtype=jnp.float32) / row_count
    row_scale = jnp.exp(jnp.log(10.0) * (0.5 * position + 0.5 * spread))
    shared = shared_part(base_key, own_key, row_count)
    rough_part = jnp.clip(jax.random.normal(jax.random.fold_in(own_key, 2), (row_count, FEAT), jnp.float32), -4.0, 4.0)
    rough_part = jnp.clip(rough_part + 0.23 * shared, -5.0, 5.0)
    overall = 0.1
    values = overall * rough_part * row_scale[:, None] * feature_scale(base_key)[None, :]
    return values.astype(jnp.bfloat16)


def draw_query_grads(key, part):
    return example_rows(key, 101, NQ)


def draw_build_grads(key, part):
    return example_rows(key, 202, NB)


def draw_scored_grads(key, part):
    return example_rows(key, 303, NS)


def setup_inputs(seed: int = 0) -> dict:
    keys = jax.random.split(jax.random.key(seed), 4)
    query_grads = draw_query_grads(jax.random.fold_in(keys[3], 71), 0)
    build_grads = draw_build_grads(jax.random.fold_in(keys[3], 71), 0)
    scored_grads = draw_scored_grads(jax.random.fold_in(keys[3], 71), 0)
    return {"query_grads": query_grads, "build_grads": build_grads, "scored_grads": scored_grads}


def reference(query_grads, build_grads, scored_grads):
    build_wide = build_grads.astype(jnp.float32)
    damping = 0.1 * jnp.sum(build_wide * build_wide) / (NB * FEAT) + 1e-06
    gram_matrix = jnp.dot(build_grads.astype(jnp.float32), build_grads.T.astype(jnp.float32), preferred_element_type=jnp.float32)
    gram_matrix = gram_matrix + NB * damping * jnp.eye(NB, dtype=jnp.float32)
    cross_sums = jnp.dot(build_grads.astype(jnp.float32), query_grads.T.astype(jnp.float32), preferred_element_type=jnp.float32)
    factor = jnp.linalg.cholesky(gram_matrix)
    solved = jax.scipy.linalg.cho_solve((factor, True), cross_sums)
    solved_half = solved.astype(jnp.bfloat16)
    query_wide = query_grads.astype(jnp.float32)
    precond = (query_wide - jnp.dot(solved_half.T.astype(jnp.float32), build_grads.astype(jnp.float32), preferred_element_type=jnp.float32)) / damping
    self_score = lax.optimization_barrier(jnp.sum(query_wide * precond, axis=1))
    normed = (precond / jnp.sqrt(self_score)[:, None]).astype(jnp.bfloat16)
    return jnp.dot(scored_grads.astype(jnp.float32), normed.T.astype(jnp.float32), preferred_element_type=jnp.float32)
```

```python
import functools

import jax
import jax.numpy as jnp
from jax import lax
from jax.experimental import pallas as pl
from jax.experimental.pallas import tpu as pltpu
from jax.sharding import PartitionSpec as P

BLOCK = 128
GROUP = 8


def contract_last(left, right):
    return lax.dot_general(
        left, right, (((1,), (1,)), ((), ())), preferred_element_type=jnp.float32
    )


def wide_dot(left, right, dims):
    return lax.dot_general(
        left,
        right,
        (dims, ((), ())),
        precision=lax.Precision.HIGHEST,
        preferred_element_type=jnp.float32,
    )


def invert_block(block):
    size = block.shape[0]
    lane = lax.broadcasted_iota(jnp.int32, (1, size), 1)
    row_id = lax.broadcasted_iota(jnp.int32, (size, 1), 0)

    def group(_, values):
        for k in range(GROUP):
            pivot = 1.0 / values[k : k + 1, k : k + 1]
            row = jnp.where(lane == k, pivot, values[k : k + 1, :] * pivot)
            column = jnp.where(row_id == k, -1.0, values[:, k : k + 1])
            base = jnp.where((lane == k) | (row_id == k), 0.0, values)
            values = base - column * row
        values = pltpu.roll(values, size - GROUP, 1)
        return jnp.concatenate([values[GROUP:], values[:GROUP]], axis=0)

    return lax.fori_loop(0, size // GROUP, group, block)


def solve_kernel(count, feature_count, tiles_ref, cross_ref, square_ref, half_ref, scale_ref, work, right):
    build_count = count * BLOCK
    place = {}
    for i in range(count):
        for j in range(i, count):
            place[i, j] = len(place)
    eye = lax.broadcasted_iota(jnp.int32, (BLOCK, BLOCK), 0) == lax.broadcasted_iota(
        jnp.int32, (BLOCK, BLOCK), 1
    )
    diagonal = jnp.zeros((BLOCK, BLOCK), jnp.float32)
    for i in range(count):
        diagonal = diagonal + jnp.where(eye, tiles_ref[place[i, i]], 0.0)
    total = jnp.sum(jnp.sum(diagonal, axis=1, keepdims=True), axis=0, keepdims=True)
    damping = 0.1 * total / (build_count * feature_count) + 1e-06
    shift = jnp.where(eye, build_count * damping, 0.0)
    for key, at in place.items():
        tile = tiles_ref[at]
        work[at] = tile + shift if key[0] == key[1] else tile
    right[...] = cross_ref[...]

    def rows(i):
        return slice(i * BLOCK, (i + 1) * BLOCK)

    for k in range(count):
        inverse = invert_block(work[place[k, k]])
        solved_right = wide_dot(inverse, right[rows(k), :], ((1,), (0,)))
        scaled = {
            j: wide_dot(inverse, work[place[k, j]], ((1,), (0,))) for j in range(k + 1, count)
        }
        for i in range(k + 1, count):
            left = work[place[k, i]]
            for j in range(i, count):
                work[place[i, j]] -= wide_dot(left, scaled[j], ((0,), (0,)))
            right[rows(i), :] -= wide_dot(left, solved_right, ((0,), (0,)))
        for j in range(k + 1, count):
            work[place[k, j]] = scaled[j]
        right[rows(k), :] = solved_right
    for k in reversed(range(count - 1)):
        value = right[rows(k), :]
        for j in range(k + 1, count):
            value = value - wide_dot(work[place[k, j]], right[rows(j), :], ((1,), (0,)))
        right[rows(k), :] = value
    half = right[...].astype(jnp.bfloat16)
    half_ref[...] = half
    kept = square_ref[...] - jnp.sum(
        half.astype(jnp.float32) * cross_ref[...], axis=0, keepdims=True
    )
    scale_ref[...] = 1.0 / jnp.sqrt(damping * kept)


def solve(tiles, cross, squares, feature_count):
    build_count, query_count = cross.shape
    count = build_count // BLOCK
    pair_count = count * (count + 1) // 2
    vmem = pl.BlockSpec(memory_space=pltpu.VMEM)
    return pl.pallas_call(
        functools.partial(solve_kernel, count, feature_count),
        out_shape=(
            jax.ShapeDtypeStruct((build_count, query_count), jnp.bfloat16),
            jax.ShapeDtypeStruct((1, query_count), jnp.float32),
        ),
        in_specs=[vmem] * 3,
        out_specs=(vmem, vmem),
        scratch_shapes=[
            pltpu.VMEM((pair_count, BLOCK, BLOCK), jnp.float32),
            pltpu.VMEM((build_count, query_count), jnp.float32),
        ],
        compiler_params=pltpu.CompilerParams(vmem_limit_bytes=48 * 1024 * 1024),
    )(tiles, cross, squares)


def scatter_sum(values, axis, parts):
    split = values.reshape((parts, values.shape[0] // parts) + values.shape[1:])
    return jnp.sum(lax.all_to_all(split, axis, 0, 0), axis=0)


def spread(values, axis, parts):
    copies = jnp.broadcast_to(values[None], (parts,) + values.shape)
    got = lax.all_to_all(copies, axis, 0, 0)
    return got.reshape((parts * values.shape[0],) + values.shape[1:])


def on_device(feat_parts, dp_parts, query_grads, build_grads, scored_grads):
    feature_count = query_grads.shape[1]
    q_shard = lax.all_to_all(query_grads, "feat", split_axis=1, concat_axis=0, tiled=True)
    q_local = lax.all_to_all(q_shard, "dp", split_axis=1, concat_axis=0, tiled=True)
    b_local = lax.all_to_all(build_grads, "dp", split_axis=1, concat_axis=0, tiled=True)
    build_count, query_count = b_local.shape[0], q_local.shape[0]
    count = build_count // BLOCK
    query_wide = q_local.astype(jnp.float32)

    strips = []
    for i in range(count):
        strip = contract_last(b_local[i * BLOCK : (i + 1) * BLOCK], b_local[i * BLOCK :])
        strips.append(strip)
    cross_part = contract_last(b_local, q_local)
    crosses = [cross_part[i * BLOCK : (i + 1) * BLOCK] for i in range(count)]
    square_part = jnp.sum(query_wide * query_wide, axis=1)
    square_rows = -(-query_count // BLOCK)
    squares_padded = jnp.zeros((square_rows * BLOCK,), jnp.float32).at[:query_count].set(square_part)
    square_tile = jnp.zeros((BLOCK, BLOCK), jnp.float32).at[:square_rows].set(
        squares_padded.reshape(square_rows, BLOCK)
    )
    wide = jnp.concatenate(strips + crosses, axis=1)
    gram_tiles = count * (count + 1) // 2
    cross_tiles = -(-count * query_count // BLOCK)
    used = gram_tiles + cross_tiles + 1
    unit = max(1, feat_parts * dp_parts // 16)
    tile_count = -(-used // unit) * unit
    pad = (gram_tiles + cross_tiles) * BLOCK - wide.shape[1]
    if pad:
        wide = jnp.pad(wide, ((0, 0), (0, pad)))
    tiles = wide.reshape(BLOCK, gram_tiles + cross_tiles, BLOCK).swapaxes(0, 1)
    tiles = jnp.concatenate(
        [tiles, square_tile[None], jnp.zeros((tile_count - used, BLOCK, BLOCK), jnp.float32)], axis=0
    )

    flat = tiles.reshape(tile_count * BLOCK, BLOCK)
    part = scatter_sum(scatter_sum(flat, "dp", dp_parts), "feat", feat_parts)
    whole = spread(spread(part, "feat", feat_parts), "dp", dp_parts)
    whole = whole.reshape(tile_count, BLOCK, BLOCK)
    cross_wide = whole[gram_tiles : gram_tiles + cross_tiles].swapaxes(0, 1).reshape(BLOCK, -1)
    cross_wide = cross_wide[:, : count * query_count].reshape(BLOCK, count, query_count)
    cross_sums = cross_wide.swapaxes(0, 1).reshape(build_count, query_count)
    squares = whole[used - 1, :square_rows].reshape(1, -1)[:, :query_count]

    solved_half, scale = solve(whole[:gram_tiles], cross_sums, squares, feature_count)

    removed = lax.dot_general(
        solved_half, b_local, (((0,), (0,)), ((), ())), preferred_element_type=jnp.float32
    )
    normed = ((query_wide - removed) * scale.reshape(-1, 1)).astype(jnp.bfloat16)
    normed = lax.all_gather(normed, "dp", axis=1, tiled=True)
    partial_value = contract_last(scored_grads, normed)
    return scatter_sum(partial_value, "feat", feat_parts)


def solution(mesh):
    placed = (P(("dp", "feat"), None), P("dp", "feat"), P("dp", "feat"))
    return jax.shard_map(
        functools.partial(on_device, mesh.shape["feat"], mesh.shape["dp"]),
        mesh=mesh,
        in_specs=placed,
        out_specs=P(("dp", "feat"), None),
        check_vma=False,
    )
```

```python
import functools

import jax
import jax.numpy as jnp
from jax import lax
from jax.experimental import pallas as pl
from jax.experimental.pallas import tpu as pltpu
from jax.sharding import PartitionSpec as P

BLOCK = 128
GROUP = 8


def contract_last(left, right):
    return lax.dot_general(
        left, right, (((1,), (1,)), ((), ())), preferred_element_type=jnp.float32
    )


def wide_dot(left, right, dims):
    return lax.dot_general(
        left,
        right,
        (dims, ((), ())),
        precision=lax.Precision.HIGHEST,
        preferred_element_type=jnp.float32,
    )


def invert_block(block):
    size = block.shape[0]
    lane = lax.broadcasted_iota(jnp.int32, (1, size), 1)
    row_id = lax.broadcasted_iota(jnp.int32, (size, 1), 0)

    def group(_, values):
        for k in range(GROUP):
            pivot = 1.0 / values[k : k + 1, k : k + 1]
            row = jnp.where(lane == k, pivot, values[k : k + 1, :] * pivot)
            column = jnp.where(row_id == k, -1.0, values[:, k : k + 1])
            base = jnp.where((lane == k) | (row_id == k), 0.0, values)
            values = base - column * row
        values = pltpu.roll(values, size - GROUP, 1)
        return jnp.concatenate([values[GROUP:], values[:GROUP]], axis=0)

    return lax.fori_loop(0, size // GROUP, group, block)


def solve_kernel(count, query_count, feature_count, tiles_ref, half_ref, scale_ref, work, cross, right):
    build_count = count * BLOCK
    place = {}
    for i in range(count):
        for j in range(i, count):
            place[i, j] = len(place)
    eye = lax.broadcasted_iota(jnp.int32, (BLOCK, BLOCK), 0) == lax.broadcasted_iota(
        jnp.int32, (BLOCK, BLOCK), 1
    )
    diagonal = jnp.zeros((BLOCK, BLOCK), jnp.float32)
    for i in range(count):
        diagonal = diagonal + jnp.where(eye, tiles_ref[place[i, i]], 0.0)
    total = jnp.sum(jnp.sum(diagonal, axis=1, keepdims=True), axis=0, keepdims=True)
    damping = 0.1 * total / (build_count * feature_count) + 1e-06
    shift = jnp.where(eye, build_count * damping, 0.0)
    for key, at in place.items():
        tile = tiles_ref[at]
        work[at] = tile + shift if key[0] == key[1] else tile
    width = right.shape[1] // BLOCK
    for i in range(count):
        for j in range(width):
            tile = tiles_ref[len(place) + i * width + j]
            cross[i * BLOCK : (i + 1) * BLOCK, j * BLOCK : (j + 1) * BLOCK] = tile
    right[...] = cross[...]

    def rows(i):
        return slice(i * BLOCK, (i + 1) * BLOCK)

    for k in range(count):
        inverse = invert_block(work[place[k, k]])
        solved_right = wide_dot(inverse, right[rows(k), :], ((1,), (0,)))
        scaled = {
            j: wide_dot(inverse, work[place[k, j]], ((1,), (0,))) for j in range(k + 1, count)
        }
        for i in range(k + 1, count):
            left = work[place[k, i]]
            for j in range(i, count):
                work[place[i, j]] -= wide_dot(left, scaled[j], ((0,), (0,)))
            right[rows(i), :] -= wide_dot(left, solved_right, ((0,), (0,)))
        for j in range(k + 1, count):
            work[place[k, j]] = scaled[j]
        right[rows(k), :] = solved_right
    for k in reversed(range(count - 1)):
        value = right[rows(k), :]
        for j in range(k + 1, count):
            value = value - wide_dot(work[place[k, j]], right[rows(j), :], ((1,), (0,)))
        right[rows(k), :] = value
    half = right[...].astype(jnp.bfloat16)
    half_ref[...] = half
    taken = jnp.sum(half.astype(jnp.float32) * cross[...], axis=0, keepdims=True)
    last = len(place) + count * width
    for j in range(width):
        lanes = slice(j * BLOCK, (j + 1) * BLOCK)
        kept = tiles_ref[last][j : j + 1, :] - taken[:, lanes]
        scale_ref[:, lanes] = 1.0 / jnp.sqrt(damping * kept)


def solve(tiles, build_count, query_count, feature_count):
    count = build_count // BLOCK
    wide = -(-query_count // BLOCK) * BLOCK
    pair_count = count * (count + 1) // 2
    vmem = pl.BlockSpec(memory_space=pltpu.VMEM)
    return pl.pallas_call(
        functools.partial(solve_kernel, count, query_count, feature_count),
        out_shape=(
            jax.ShapeDtypeStruct((build_count, wide), jnp.bfloat16),
            jax.ShapeDtypeStruct((1, wide), jnp.float32),
        ),
        in_specs=[vmem],
        out_specs=(vmem, vmem),
        scratch_shapes=[
            pltpu.VMEM((pair_count, BLOCK, BLOCK), jnp.float32),
            pltpu.VMEM((build_count, wide), jnp.float32),
            pltpu.VMEM((build_count, wide), jnp.float32),
        ],
        compiler_params=pltpu.CompilerParams(vmem_limit_bytes=48 * 1024 * 1024),
    )(tiles)


MESH = pl.DeviceIdType.MESH


def scatter_sum(values, axis, parts):
    split = values.reshape((parts, values.shape[0] // parts) + values.shape[1:])
    return jnp.sum(lax.all_to_all(split, axis, 0, 0), axis=0)


def exchange_kernel(
    feat_parts, dp_parts, query_ref, build_ref, query_out, build_out,
    local_sem, query_send, query_recv, build_send, build_recv,
):
    feat, dp = lax.axis_index("feat"), lax.axis_index("dp")
    parts = feat_parts * dp_parts
    me = dp * feat_parts + feat
    rows, span = build_ref.shape[0], build_out.shape[1]

    def peer(step):
        at = lax.rem(me + step, parts)
        return at, {"dp": at // feat_parts, "feat": lax.rem(at, feat_parts)}

    barrier = pltpu.get_barrier_semaphore()

    def greet(step, _):
        pl.semaphore_signal(barrier, inc=1, device_id=peer(step)[1], device_id_type=MESH)
        return 0

    lax.fori_loop(1, parts, greet, 0)
    pl.semaphore_wait(barrier, parts - 1)

    def query_copy(step):
        at, device = peer(step)
        return pltpu.make_async_remote_copy(
            src_ref=query_ref.at[at],
            dst_ref=query_out.at[me],
            send_sem=query_send.at[step],
            recv_sem=query_recv.at[step],
            device_id=device,
            device_id_type=MESH,
        )

    def columns(owner):
        return pl.ds(pl.multiple_of(owner * span, BLOCK), span)

    mine = pl.ds(pl.multiple_of(dp * rows, 16), rows)
    own = [
        pltpu.make_async_copy(build_ref.at[:, columns(dp)], build_out.at[mine], local_sem.at[0]),
        pltpu.make_async_copy(query_ref.at[me], query_out.at[me], local_sem.at[1]),
    ]
    sent = []
    for step in range(1, dp_parts):
        target = lax.rem(dp + step, dp_parts)
        sent.append(
            pltpu.make_async_remote_copy(
                src_ref=build_ref.at[:, columns(target)],
                dst_ref=build_out.at[mine],
                send_sem=build_send.at[step],
                recv_sem=build_recv.at[step],
                device_id={"dp": target, "feat": feat},
                device_id_type=MESH,
            )
        )

    def start_query(step, _):
        query_copy(step).start()
        return 0

    lax.fori_loop(1, parts, start_query, 0)
    for copy in sent + own:
        copy.start()

    def wait_query(step, _):
        query_copy(step).wait()
        return 0

    lax.fori_loop(1, parts, wait_query, 0)
    for copy in sent + own:
        copy.wait()


def exchange(query_grads, build_grads, feat_parts, dp_parts):
    parts = feat_parts * dp_parts
    rows, features = query_grads.shape
    span = features // parts
    arranged = query_grads.reshape(rows, feat_parts, dp_parts, span).transpose(2, 1, 0, 3)
    arranged = arranged.reshape(parts, rows * span // BLOCK, BLOCK)
    anywhere = pl.BlockSpec(memory_space=pl.ANY)
    query_out, build_out = pl.pallas_call(
        functools.partial(exchange_kernel, feat_parts, dp_parts),
        out_shape=(
            jax.ShapeDtypeStruct(arranged.shape, jnp.bfloat16),
            jax.ShapeDtypeStruct((build_grads.shape[0] * dp_parts, span), jnp.bfloat16),
        ),
        in_specs=[anywhere] * 2,
        out_specs=(anywhere, anywhere),
        scratch_shapes=[
            pltpu.SemaphoreType.DMA((2,)),
            pltpu.SemaphoreType.DMA((parts,)),
            pltpu.SemaphoreType.DMA((parts,)),
            pltpu.SemaphoreType.DMA((dp_parts,)),
            pltpu.SemaphoreType.DMA((dp_parts,)),
        ],
        compiler_params=pltpu.CompilerParams(collective_id=0, has_side_effects=True),
    )(arranged, build_grads)
    return query_out.reshape(rows * parts, span), build_out


def gram_kernel(query_ref, build_ref, out_ref, gram, cross, square):
    build_count, features = build_ref.shape
    query_count = query_ref.shape[0]
    count = build_count // BLOCK
    step = min(512, features)
    strip = 2 * BLOCK if count % 2 == 0 else BLOCK
    gram[...] = jnp.zeros_like(gram)
    cross[...] = jnp.zeros_like(cross)
    square[...] = jnp.zeros_like(square)

    @pl.loop(0, features // step)
    def _(at):
        here = pl.ds(pl.multiple_of(at * step, BLOCK), step)
        build = build_ref[:, here]
        query = query_ref[:, here]
        for low in range(0, build_count, strip):
            gram[low : low + strip, low:] += contract_last(build[low : low + strip], build[low:])
        cross[:, :query_count] += contract_last(build, query)
        wide = query.astype(jnp.float32)
        square[...] += jnp.sum(wide * wide, axis=1, keepdims=True)

    place = 0
    for i in range(count):
        for j in range(i, count):
            out_ref[pl.ds(place * BLOCK, BLOCK), :] = gram[
                i * BLOCK : (i + 1) * BLOCK, j * BLOCK : (j + 1) * BLOCK
            ]
            place += 1
    width = cross.shape[1] // BLOCK
    for i in range(count):
        for j in range(width):
            out_ref[pl.ds(place * BLOCK, BLOCK), :] = cross[
                i * BLOCK : (i + 1) * BLOCK, j * BLOCK : (j + 1) * BLOCK
            ]
            place += 1
    out_ref[pl.ds(place * BLOCK, out_ref.shape[0] - place * BLOCK), :] = jnp.zeros(
        (out_ref.shape[0] - place * BLOCK, BLOCK), jnp.float32
    )
    for j in range(-(-query_count // BLOCK)):
        size = min(BLOCK, query_count - j * BLOCK)
        eye = lax.broadcasted_iota(jnp.int32, (size, BLOCK), 0) == lax.broadcasted_iota(
            jnp.int32, (size, BLOCK), 1
        )
        column = square[j * BLOCK : j * BLOCK + size, :]
        row = jnp.sum(jnp.where(eye, column, 0.0), axis=0, keepdims=True)
        out_ref[pl.ds(place * BLOCK + j, 1), :] = row


def gram_tiles(query_local, build_local, tile_count):
    build_count, query_count = build_local.shape[0], query_local.shape[0]
    wide = -(-query_count // BLOCK) * BLOCK
    vmem = pl.BlockSpec(memory_space=pltpu.VMEM)
    return pl.pallas_call(
        gram_kernel,
        out_shape=jax.ShapeDtypeStruct((tile_count * BLOCK, BLOCK), jnp.float32),
        in_specs=[vmem] * 2,
        out_specs=vmem,
        scratch_shapes=[
            pltpu.VMEM((build_count, build_count), jnp.float32),
            pltpu.VMEM((build_count, wide), jnp.float32),
            pltpu.VMEM((query_count, 1), jnp.float32),
        ],
        compiler_params=pltpu.CompilerParams(vmem_limit_bytes=48 * 1024 * 1024),
    )(query_local, build_local)


def sum_kernel(
    feat_parts, dp_parts, values_ref, whole_ref,
    pair_in, pair_sum, chip_in, chip_sum, feat_in, send_sem, recv_sem,
):
    feat, dp = lax.axis_index("feat"), lax.axis_index("dp")
    chips = dp_parts // 2
    core, chip = lax.rem(dp, 2), dp // 2
    total = values_ref.shape[0]
    half, quarter, piece = total // 2, total // dp_parts, total // (dp_parts * feat_parts)

    def part(start, size):
        return pl.ds(pl.multiple_of(start, 8), size)

    other = {"dp": chip * 2 + 1 - core, "feat": feat}

    def along_chips(step):
        at = lax.rem(chip + step, chips)
        return at, {"dp": at * 2 + core, "feat": feat}

    def along_feat(step):
        at = lax.rem(feat + step, feat_parts)
        return at, {"dp": dp, "feat": at}

    barrier = pltpu.get_barrier_semaphore()
    peers = [other]
    peers += [along_chips(step)[1] for step in range(1, chips)]
    peers += [along_feat(step)[1] for step in range(1, feat_parts)]
    for device in peers:
        pl.semaphore_signal(barrier, inc=1, device_id=device, device_id_type=MESH)
    pl.semaphore_wait(barrier, len(peers))

    used = [0]

    def send(source, target, device):
        copy = pltpu.make_async_remote_copy(
            src_ref=source,
            dst_ref=target,
            send_sem=send_sem.at[used[0]],
            recv_sem=recv_sem.at[used[0]],
            device_id=device,
            device_id_type=MESH,
        )
        used[0] += 1
        copy.start()
        return copy

    send(values_ref.at[part((1 - core) * half, half)], pair_in, other).wait()
    pair_sum[...] = values_ref[part(core * half, half), :] + pair_in[...]

    copies = []
    for step in range(1, chips):
        at, device = along_chips(step)
        copies.append(send(pair_sum.at[part(at * quarter, quarter)], chip_in.at[step - 1], device))
    value = pair_sum[part(chip * quarter, quarter), :]
    for step, copy in enumerate(copies):
        copy.wait()
        value = value + chip_in[step]
    chip_sum[...] = value

    copies = []
    for step in range(1, feat_parts):
        at, device = along_feat(step)
        copies.append(send(chip_sum.at[part(at * piece, piece)], feat_in.at[step - 1], device))
    value = chip_sum[part(feat * piece, piece), :]
    for step, copy in enumerate(copies):
        copy.wait()
        value = value + feat_in[step]

    base = core * half + chip * quarter
    mine = whole_ref.at[part(base + feat * piece, piece)]
    mine[...] = value
    copies = [send(mine, mine, along_feat(step)[1]) for step in range(1, feat_parts)]
    for copy in copies:
        copy.wait()
    mine = whole_ref.at[part(base, quarter)]
    copies = [send(mine, mine, along_chips(step)[1]) for step in range(1, chips)]
    for copy in copies:
        copy.wait()
    mine = whole_ref.at[part(core * half, half)]
    send(mine, mine, other).wait()


def sum_everywhere(values, feat_parts, dp_parts):
    total = values.shape[0]
    chips = dp_parts // 2
    quarter, piece = total // dp_parts, total // (dp_parts * feat_parts)
    copies = 2 * (1 + (chips - 1) + (feat_parts - 1))
    vmem = pl.BlockSpec(memory_space=pltpu.VMEM)
    return pl.pallas_call(
        functools.partial(sum_kernel, feat_parts, dp_parts),
        out_shape=jax.ShapeDtypeStruct(values.shape, jnp.float32),
        in_specs=[vmem],
        out_specs=vmem,
        scratch_shapes=[
            pltpu.VMEM((total // 2, BLOCK), jnp.float32),
            pltpu.VMEM((total // 2, BLOCK), jnp.float32),
            pltpu.VMEM((max(1, chips - 1), quarter, BLOCK), jnp.float32),
            pltpu.VMEM((quarter, BLOCK), jnp.float32),
            pltpu.VMEM((max(1, feat_parts - 1), piece, BLOCK), jnp.float32),
            pltpu.SemaphoreType.DMA((copies,)),
            pltpu.SemaphoreType.DMA((copies,)),
        ],
        compiler_params=pltpu.CompilerParams(
            collective_id=1, has_side_effects=True, vmem_limit_bytes=48 * 1024 * 1024
        ),
    )(values)


def on_device(feat_parts, dp_parts, query_grads, build_grads, scored_grads):
    feature_count = query_grads.shape[1]
    q_local, b_local = exchange(query_grads, build_grads, feat_parts, dp_parts)
    build_count, query_count = b_local.shape[0], q_local.shape[0]
    count, width = build_count // BLOCK, -(-query_count // BLOCK)
    used = count * (count + 1) // 2 + count * width + 1
    unit = max(1, feat_parts * dp_parts // 16)
    tile_count = -(-used // unit) * unit
    tiles = gram_tiles(q_local, b_local, tile_count)
    whole = sum_everywhere(tiles, feat_parts, dp_parts).reshape(tile_count, BLOCK, BLOCK)
    solved_half, scale = solve(whole, build_count, query_count, feature_count)
    query_wide = q_local.astype(jnp.float32)
    removed = lax.dot_general(
        solved_half[:, :query_count], b_local, (((0,), (0,)), ((), ())),
        preferred_element_type=jnp.float32,
    )
    normed = ((query_wide - removed) * scale[:, :query_count].reshape(-1, 1)).astype(jnp.bfloat16)
    normed = lax.all_gather(normed, "dp", axis=1, tiled=True)
    partial_value = contract_last(scored_grads, normed)
    return scatter_sum(partial_value, "feat", feat_parts)


def solution(mesh):
    placed = (P(("dp", "feat"), None), P("dp", "feat"), P("dp", "feat"))
    return jax.shard_map(
        functools.partial(on_device, mesh.shape["feat"], mesh.shape["dp"]),
        mesh=mesh,
        in_specs=placed,
        out_specs=P(("dp", "feat"), None),
        check_vma=False,
    )
```

```python
import functools

import jax
import jax.numpy as jnp
from jax import lax
from jax.experimental import pallas as pl
from jax.experimental.pallas import tpu as pltpu
from jax.sharding import PartitionSpec as P

BLOCK = 128
GROUP = 8


def contract_last(left, right):
    return lax.dot_general(
        left, right, (((1,), (1,)), ((), ())), preferred_element_type=jnp.float32
    )


def wide_dot(left, right, dims):
    return lax.dot_general(
        left,
        right,
        (dims, ((), ())),
        precision=lax.Precision.HIGHEST,
        preferred_element_type=jnp.float32,
    )


def invert_block(block):
    size = block.shape[0]
    lane = lax.broadcasted_iota(jnp.int32, (1, size), 1)
    row_id = lax.broadcasted_iota(jnp.int32, (GROUP, 1), 0)

    def group(_, values):
        top, rest = values[:GROUP], values[GROUP:]
        for k in range(0, GROUP, 2):
            first, second = lane == k, lane == k + 1
            top_0, top_1 = top[:, k : k + 1], top[:, k + 1 : k + 2]
            rest_0, rest_1 = rest[:, k : k + 1], rest[:, k + 1 : k + 2]
            corner, upper = top_0[k : k + 1], top_1[k : k + 1]
            lower, other = top_0[k + 1 : k + 2], top_1[k + 1 : k + 2]
            inverse = 1.0 / (corner * other - upper * lower)
            row_0 = jnp.where(first, 1.0, jnp.where(second, 0.0, top[k : k + 1]))
            row_1 = jnp.where(first, 0.0, jnp.where(second, 1.0, top[k + 1 : k + 2]))
            new_0 = (other * row_0 - upper * row_1) * inverse
            new_1 = (corner * row_1 - lower * row_0) * inverse
            both = first | second
            at_0, at_1 = row_id == k, row_id == k + 1
            top_0 = jnp.where(at_0, -1.0, jnp.where(at_1, 0.0, top_0))
            top_1 = jnp.where(at_1, -1.0, jnp.where(at_0, 0.0, top_1))
            top = jnp.where(both | at_0 | at_1, 0.0, top) - top_0 * new_0 - top_1 * new_1
            rest = jnp.where(both, 0.0, rest) - rest_0 * new_0 - rest_1 * new_1
        return pltpu.roll(jnp.concatenate([rest, top], axis=0), size - GROUP, 1)

    return lax.fori_loop(0, size // GROUP, group, block)


def solve_kernel(count, feature_count, tiles_ref, half_ref, scale_ref, right, *strips):
    build_count = count * BLOCK
    width = right.shape[1] // BLOCK
    place = {}
    for i in range(count):
        for j in range(i, count):
            place[i, j] = len(place)
    eye = lax.broadcasted_iota(jnp.int32, (BLOCK, BLOCK), 0) == lax.broadcasted_iota(
        jnp.int32, (BLOCK, BLOCK), 1
    )
    diagonal = jnp.zeros((BLOCK, BLOCK), jnp.float32)
    for i in range(count):
        diagonal = diagonal + jnp.where(eye, tiles_ref[place[i, i]], 0.0)
    total = jnp.sum(jnp.sum(diagonal, axis=1, keepdims=True), axis=0, keepdims=True)
    damping = 0.1 * total / (build_count * feature_count) + 1e-06
    shift = jnp.where(eye, build_count * damping, 0.0)

    def lanes(i):
        return slice(i * BLOCK, (i + 1) * BLOCK)

    for i in range(count):
        for j in range(i, count):
            tile = tiles_ref[place[i, j]]
            strips[i][:, lanes(j - i)] = tile + shift if i == j else tile
        for j in range(width):
            strips[i][:, lanes(count - i + j)] = tiles_ref[len(place) + i * width + j]

    for k in range(count):
        inverse = invert_block(strips[k][:, :BLOCK])
        scaled = wide_dot(inverse, strips[k][:, BLOCK:], ((1,), (0,)))
        for i in range(k + 1, count):
            left = strips[k][:, lanes(i - k)]
            strips[i][...] -= wide_dot(left, scaled[:, (i - k - 1) * BLOCK :], ((0,), (0,)))
        strips[k][:, BLOCK:] = scaled
    for k in reversed(range(count)):
        end = (count - k) * BLOCK
        value = strips[k][:, end:]
        if k + 1 < count:
            value = value - wide_dot(
                strips[k][:, BLOCK:end], right[(k + 1) * BLOCK :, :], ((1,), (0,))
            )
        right[k * BLOCK : (k + 1) * BLOCK, :] = value
    half = right[...].astype(jnp.bfloat16)
    half_ref[...] = half
    last = len(place) + count * width
    for j in range(width):
        taken = jnp.zeros((1, BLOCK), jnp.float32)
        for i in range(count):
            block = half[lanes(i), lanes(j)].astype(jnp.float32)
            taken = taken + jnp.sum(
                block * tiles_ref[len(place) + i * width + j], axis=0, keepdims=True
            )
        kept = tiles_ref[last][j : j + 1, :] - taken
        scale_ref[:, lanes(j)] = 1.0 / jnp.sqrt(damping * kept)


def solve(tiles, build_count, query_count, feature_count):
    count = build_count // BLOCK
    wide = -(-query_count // BLOCK) * BLOCK
    vmem = pl.BlockSpec(memory_space=pltpu.VMEM)
    return pl.pallas_call(
        functools.partial(solve_kernel, count, feature_count),
        out_shape=(
            jax.ShapeDtypeStruct((build_count, wide), jnp.bfloat16),
            jax.ShapeDtypeStruct((1, wide), jnp.float32),
        ),
        in_specs=[vmem],
        out_specs=(vmem, vmem),
        scratch_shapes=[pltpu.VMEM((build_count, wide), jnp.float32)]
        + [pltpu.VMEM((BLOCK, (count - k) * BLOCK + wide), jnp.float32) for k in range(count)],
        compiler_params=pltpu.CompilerParams(vmem_limit_bytes=48 * 1024 * 1024),
    )(tiles)


MESH = pl.DeviceIdType.MESH


def exchange_kernel(
    feat_parts, dp_parts, query_ref, build_ref, query_out, build_out,
    local_sem, query_send, query_recv, build_send, build_recv,
):
    feat, dp = lax.axis_index("feat"), lax.axis_index("dp")
    parts = feat_parts * dp_parts
    me = dp * feat_parts + feat
    rows, span = build_ref.shape[0], build_out.shape[1]

    def peer(step):
        at = lax.rem(me + step, parts)
        return at, {"dp": at // feat_parts, "feat": lax.rem(at, feat_parts)}

    barrier = pltpu.get_barrier_semaphore()

    def greet(step, _):
        pl.semaphore_signal(barrier, inc=1, device_id=peer(step)[1], device_id_type=MESH)
        return 0

    lax.fori_loop(1, parts, greet, 0)
    pl.semaphore_wait(barrier, parts - 1)

    def query_copy(step):
        at, device = peer(step)
        return pltpu.make_async_remote_copy(
            src_ref=query_ref.at[at],
            dst_ref=query_out.at[me],
            send_sem=query_send.at[step],
            recv_sem=query_recv.at[step],
            device_id=device,
            device_id_type=MESH,
        )

    def columns(owner):
        return pl.ds(pl.multiple_of(owner * span, BLOCK), span)

    mine = pl.ds(pl.multiple_of(dp * rows, 16), rows)
    own = [
        pltpu.make_async_copy(build_ref.at[:, columns(dp)], build_out.at[mine], local_sem.at[0]),
        pltpu.make_async_copy(query_ref.at[me], query_out.at[me], local_sem.at[1]),
    ]
    sent = []
    for step in range(1, dp_parts):
        target = lax.rem(dp + step, dp_parts)
        sent.append(
            pltpu.make_async_remote_copy(
                src_ref=build_ref.at[:, columns(target)],
                dst_ref=build_out.at[mine],
                send_sem=build_send.at[step],
                recv_sem=build_recv.at[step],
                device_id={"dp": target, "feat": feat},
                device_id_type=MESH,
            )
        )

    def start_query(step, _):
        query_copy(step).start()
        return 0

    lax.fori_loop(1, parts, start_query, 0)
    for copy in sent + own:
        copy.start()

    def wait_query(step, _):
        query_copy(step).wait()
        return 0

    lax.fori_loop(1, parts, wait_query, 0)
    for copy in sent + own:
        copy.wait()


def exchange(query_grads, build_grads, feat_parts, dp_parts):
    parts = feat_parts * dp_parts
    rows, features = query_grads.shape
    span = features // parts
    arranged = query_grads.reshape(rows, feat_parts, dp_parts, span).transpose(2, 1, 0, 3)
    arranged = arranged.reshape(parts, rows * span // BLOCK, BLOCK)
    anywhere = pl.BlockSpec(memory_space=pl.ANY)
    query_out, build_out = pl.pallas_call(
        functools.partial(exchange_kernel, feat_parts, dp_parts),
        out_shape=(
            jax.ShapeDtypeStruct(arranged.shape, jnp.bfloat16),
            jax.ShapeDtypeStruct((build_grads.shape[0] * dp_parts, span), jnp.bfloat16),
        ),
        in_specs=[anywhere] * 2,
        out_specs=(anywhere, anywhere),
        scratch_shapes=[
            pltpu.SemaphoreType.DMA((2,)),
            pltpu.SemaphoreType.DMA((parts,)),
            pltpu.SemaphoreType.DMA((parts,)),
            pltpu.SemaphoreType.DMA((dp_parts,)),
            pltpu.SemaphoreType.DMA((dp_parts,)),
        ],
        compiler_params=pltpu.CompilerParams(collective_id=0, has_side_effects=True),
    )(arranged, build_grads)
    return query_out.reshape(rows * parts, span), build_out


def gram_kernel(query_ref, build_ref, out_ref, gram, cross, square):
    build_count, features = build_ref.shape
    query_count = query_ref.shape[0]
    count = build_count // BLOCK
    step = min(512, features)
    strip = 2 * BLOCK if count % 2 == 0 else BLOCK
    gram[...] = jnp.zeros_like(gram)
    cross[...] = jnp.zeros_like(cross)
    square[...] = jnp.zeros_like(square)

    @pl.loop(0, features // step)
    def _(at):
        here = pl.ds(pl.multiple_of(at * step, BLOCK), step)
        build = build_ref[:, here]
        query = query_ref[:, here]
        for low in range(0, build_count, strip):
            gram[low : low + strip, low:] += contract_last(build[low : low + strip], build[low:])
        cross[:, :query_count] += contract_last(build, query)
        wide = query.astype(jnp.float32)
        square[...] += jnp.sum(wide * wide, axis=1, keepdims=True)

    place = 0
    for i in range(count):
        for j in range(i, count):
            out_ref[pl.ds(place * BLOCK, BLOCK), :] = gram[
                i * BLOCK : (i + 1) * BLOCK, j * BLOCK : (j + 1) * BLOCK
            ]
            place += 1
    width = cross.shape[1] // BLOCK
    for i in range(count):
        for j in range(width):
            out_ref[pl.ds(place * BLOCK, BLOCK), :] = cross[
                i * BLOCK : (i + 1) * BLOCK, j * BLOCK : (j + 1) * BLOCK
            ]
            place += 1
    out_ref[pl.ds(place * BLOCK, out_ref.shape[0] - place * BLOCK), :] = jnp.zeros(
        (out_ref.shape[0] - place * BLOCK, BLOCK), jnp.float32
    )
    for j in range(-(-query_count // BLOCK)):
        size = min(BLOCK, query_count - j * BLOCK)
        eye = lax.broadcasted_iota(jnp.int32, (size, BLOCK), 0) == lax.broadcasted_iota(
            jnp.int32, (size, BLOCK), 1
        )
        column = square[j * BLOCK : j * BLOCK + size, :]
        row = jnp.sum(jnp.where(eye, column, 0.0), axis=0, keepdims=True)
        out_ref[pl.ds(place * BLOCK + j, 1), :] = row


def gram_tiles(query_local, build_local, tile_count):
    build_count, query_count = build_local.shape[0], query_local.shape[0]
    wide = -(-query_count // BLOCK) * BLOCK
    vmem = pl.BlockSpec(memory_space=pltpu.VMEM)
    return pl.pallas_call(
        gram_kernel,
        out_shape=jax.ShapeDtypeStruct((tile_count * BLOCK, BLOCK), jnp.float32),
        in_specs=[vmem] * 2,
        out_specs=vmem,
        scratch_shapes=[
            pltpu.VMEM((build_count, build_count), jnp.float32),
            pltpu.VMEM((build_count, wide), jnp.float32),
            pltpu.VMEM((query_count, 1), jnp.float32),
        ],
        compiler_params=pltpu.CompilerParams(vmem_limit_bytes=48 * 1024 * 1024),
    )(query_local, build_local)


def sum_kernel(
    feat_parts, dp_parts, values_ref, whole_ref,
    pair_in, pair_sum, chip_in, chip_sum, feat_in, send_sem, recv_sem,
):
    feat, dp = lax.axis_index("feat"), lax.axis_index("dp")
    chips = dp_parts // 2
    core, chip = lax.rem(dp, 2), dp // 2
    total = values_ref.shape[0]
    half, quarter, piece = total // 2, total // dp_parts, total // (dp_parts * feat_parts)

    def part(start, size):
        return pl.ds(pl.multiple_of(start, 8), size)

    other = {"dp": chip * 2 + 1 - core, "feat": feat}

    def along_chips(step):
        at = lax.rem(chip + step, chips)
        return at, {"dp": at * 2 + core, "feat": feat}

    def along_feat(step):
        at = lax.rem(feat + step, feat_parts)
        return at, {"dp": dp, "feat": at}

    barrier = pltpu.get_barrier_semaphore()
    peers = [other]
    peers += [along_chips(step)[1] for step in range(1, chips)]
    peers += [along_feat(step)[1] for step in range(1, feat_parts)]
    for device in peers:
        pl.semaphore_signal(barrier, inc=1, device_id=device, device_id_type=MESH)
    pl.semaphore_wait(barrier, len(peers))

    used = [0]

    def send(source, target, device):
        copy = pltpu.make_async_remote_copy(
            src_ref=source,
            dst_ref=target,
            send_sem=send_sem.at[used[0]],
            recv_sem=recv_sem.at[used[0]],
            device_id=device,
            device_id_type=MESH,
        )
        used[0] += 1
        copy.start()
        return copy

    send(values_ref.at[part((1 - core) * half, half)], pair_in, other).wait()
    pair_sum[...] = values_ref[part(core * half, half), :] + pair_in[...]

    copies = []
    for step in range(1, chips):
        at, device = along_chips(step)
        copies.append(send(pair_sum.at[part(at * quarter, quarter)], chip_in.at[step - 1], device))
    value = pair_sum[part(chip * quarter, quarter), :]
    for step, copy in enumerate(copies):
        copy.wait()
        value = value + chip_in[step]
    chip_sum[...] = value

    copies = []
    for step in range(1, feat_parts):
        at, device = along_feat(step)
        copies.append(send(chip_sum.at[part(at * piece, piece)], feat_in.at[step - 1], device))
    value = chip_sum[part(feat * piece, piece), :]
    for step, copy in enumerate(copies):
        copy.wait()
        value = value + feat_in[step]

    base = core * half + chip * quarter
    mine = whole_ref.at[part(base + feat * piece, piece)]
    mine[...] = value
    copies = [send(mine, mine, along_feat(step)[1]) for step in range(1, feat_parts)]
    for copy in copies:
        copy.wait()
    mine = whole_ref.at[part(base, quarter)]
    copies = [send(mine, mine, along_chips(step)[1]) for step in range(1, chips)]
    for copy in copies:
        copy.wait()
    mine = whole_ref.at[part(core * half, half)]
    send(mine, mine, other).wait()


def sum_everywhere(values, feat_parts, dp_parts):
    total = values.shape[0]
    chips = dp_parts // 2
    quarter, piece = total // dp_parts, total // (dp_parts * feat_parts)
    copies = 2 * (1 + (chips - 1) + (feat_parts - 1))
    vmem = pl.BlockSpec(memory_space=pltpu.VMEM)
    return pl.pallas_call(
        functools.partial(sum_kernel, feat_parts, dp_parts),
        out_shape=jax.ShapeDtypeStruct(values.shape, jnp.float32),
        in_specs=[vmem],
        out_specs=vmem,
        scratch_shapes=[
            pltpu.VMEM((total // 2, BLOCK), jnp.float32),
            pltpu.VMEM((total // 2, BLOCK), jnp.float32),
            pltpu.VMEM((max(1, chips - 1), quarter, BLOCK), jnp.float32),
            pltpu.VMEM((quarter, BLOCK), jnp.float32),
            pltpu.VMEM((max(1, feat_parts - 1), piece, BLOCK), jnp.float32),
            pltpu.SemaphoreType.DMA((copies,)),
            pltpu.SemaphoreType.DMA((copies,)),
        ],
        compiler_params=pltpu.CompilerParams(
            collective_id=1, has_side_effects=True, vmem_limit_bytes=48 * 1024 * 1024
        ),
    )(values)


def score_kernel(
    feat_parts, dp_parts, half_ref, scale_ref, query_ref, build_ref, scored_ref, out_ref,
    normed, scored, total, packed, arrived,
    load_sem, pair_send, pair_recv, chip_send, chip_recv, pass_send, pass_recv, feat_send, feat_recv,
):
    feat, dp = lax.axis_index("feat"), lax.axis_index("dp")
    chips = dp_parts // 2
    core, chip = lax.rem(dp, 2), dp // 2
    query_count, span = query_ref.shape
    rows = scored_ref.shape[0]
    pieces = normed.shape[0] // dp_parts
    size = span // pieces
    other = {"dp": chip * 2 + 1 - core, "feat": feat}

    def along_chips(step):
        return {"dp": lax.rem(chip + step, chips) * 2 + core, "feat": feat}

    def from_chip(step):
        return lax.rem(chip + chips - step, chips) * 2

    def along_feat(step):
        at = lax.rem(feat + step, feat_parts)
        return at, {"dp": dp, "feat": at}

    loads = []
    owners = [dp, chip * 2 + 1 - core]
    for step in range(1, chips):
        owners += [from_chip(step) + core, from_chip(step) + 1 - core]
    for at, owner in enumerate(owners):
        columns = pl.ds(pl.multiple_of(owner * span, BLOCK), span)
        load = pltpu.make_async_copy(scored_ref.at[:, columns], scored.at[at], load_sem.at[at])
        load.start()
        loads.append(load)

    peers = [other] + [along_chips(step) for step in range(1, chips)]
    peers += [along_feat(step)[1] for step in range(1, feat_parts)]
    barrier = pltpu.get_barrier_semaphore()
    for device in peers:
        pl.semaphore_signal(barrier, inc=1, device_id=device, device_id_type=MESH)
    pl.semaphore_wait(barrier, len(peers))

    def send(slot, device, send_sem, recv_sem):
        return pltpu.make_async_remote_copy(
            src_ref=normed.at[slot],
            dst_ref=normed.at[slot],
            send_sem=send_sem,
            recv_sem=recv_sem,
            device_id=device,
            device_id_type=MESH,
        )

    half = half_ref[:, :query_count]
    scale_row = scale_ref[:, :query_count]
    eye = lax.broadcasted_iota(jnp.int32, (query_count, query_count), 0) == lax.broadcasted_iota(
        jnp.int32, (query_count, query_count), 1
    )
    scale = jnp.sum(jnp.where(eye, scale_row, 0.0), axis=1, keepdims=True)
    sent, pairs, chip_copies = [], [], {}
    for piece in range(pieces):
        here = slice(piece * size, (piece + 1) * size)
        removed = lax.dot_general(
            half, build_ref[:, here], (((0,), (0,)), ((), ())), preferred_element_type=jnp.float32
        )
        value = (query_ref[:, here].astype(jnp.float32) - removed) * scale
        normed[dp * pieces + piece] = value.astype(jnp.bfloat16)
        for step in range(1, chips):
            at = (step - 1) * pieces + piece
            copy = send(dp * pieces + piece, along_chips(step), chip_send.at[at], chip_recv.at[at])
            copy.start()
            chip_copies[step, piece] = copy
        copy = send(dp * pieces + piece, other, pair_send.at[piece], pair_recv.at[piece])
        copy.start()
        pairs.append(copy)

    total[...] = jnp.zeros_like(total)

    def multiply(at, piece):
        left = scored.at[at]
        right = normed.at[owners[at] * pieces + piece]

        @pl.loop(0, rows // BLOCK)
        def _(row):
            here = pl.ds(pl.multiple_of(row * BLOCK, BLOCK), BLOCK)
            total[here, :] += contract_last(
                left[here, piece * size : (piece + 1) * size], right[...]
            )

    loads[0].wait()
    for piece in range(pieces):
        multiply(0, piece)
    loads[1].wait()
    for piece in range(pieces):
        pairs[piece].wait_recv()
        multiply(1, piece)
    passed = []
    for step in range(1, chips):
        loads[2 * step].wait()
        loads[2 * step + 1].wait()
    for piece in range(pieces):
        for step in range(1, chips):
            at = (step - 1) * pieces + piece
            chip_copies[step, piece].wait_recv()
            copy = send(
                (from_chip(step) + core) * pieces + piece, other, pass_send.at[at], pass_recv.at[at]
            )
            copy.start()
            multiply(2 * step, piece)
            copy.wait_recv()
            multiply(2 * step + 1, piece)
            passed.append(copy)
    for copy in pairs + list(chip_copies.values()) + passed:
        copy.wait_send()

    share = rows // feat_parts
    fold = packed.shape[2] // query_count
    part = share // fold
    for owner in range(feat_parts):
        blocks = [
            total[owner * share + at * part : owner * share + (at + 1) * part, :]
            for at in range(fold)
        ]
        packed[owner] = blocks[0] if fold == 1 else jnp.concatenate(blocks, axis=1)
    copies = []
    for step in range(1, feat_parts):
        at, device = along_feat(step)
        copy = pltpu.make_async_remote_copy(
            src_ref=packed.at[at],
            dst_ref=arrived.at[step - 1],
            send_sem=feat_send.at[step],
            recv_sem=feat_recv.at[step],
            device_id=device,
            device_id_type=MESH,
        )
        copy.start()
        copies.append(copy)
    value = packed[feat]
    for step, copy in enumerate(copies):
        copy.wait()
        value = value + arrived[step]
    for at in range(fold):
        out_ref[at * part : (at + 1) * part, :] = value[
            :, at * query_count : (at + 1) * query_count
        ]


def score(solved_half, scale, query_local, build_local, scored_grads, feat_parts, dp_parts):
    query_count, span = query_local.shape
    rows = scored_grads.shape[0]
    pieces = 2 if span % (2 * BLOCK) == 0 else 1
    chips = dp_parts // 2
    share = rows // feat_parts
    fold = BLOCK // query_count if query_count < BLOCK and share % (8 * BLOCK // query_count) == 0 else 1
    vmem = pl.BlockSpec(memory_space=pltpu.VMEM)
    remote = max(1, (chips - 1) * pieces)
    dma = pltpu.SemaphoreType.DMA
    return pl.pallas_call(
        functools.partial(score_kernel, feat_parts, dp_parts),
        out_shape=jax.ShapeDtypeStruct((share, query_count), jnp.float32),
        in_specs=[vmem] * 4 + [pl.BlockSpec(memory_space=pl.ANY)],
        out_specs=vmem,
        scratch_shapes=[
            pltpu.VMEM((dp_parts * pieces, query_count, span // pieces), jnp.bfloat16),
            pltpu.VMEM((dp_parts, rows, span), jnp.bfloat16),
            pltpu.VMEM((rows, query_count), jnp.float32),
            pltpu.VMEM((feat_parts, share // fold, query_count * fold), jnp.float32),
            pltpu.VMEM((max(1, feat_parts - 1), share // fold, query_count * fold), jnp.float32),
            dma((dp_parts,)),
            dma((pieces,)),
            dma((pieces,)),
            dma((remote,)),
            dma((remote,)),
            dma((remote,)),
            dma((remote,)),
            dma((feat_parts,)),
            dma((feat_parts,)),
        ],
        compiler_params=pltpu.CompilerParams(
            collective_id=2, has_side_effects=True, vmem_limit_bytes=48 * 1024 * 1024
        ),
    )(solved_half, scale, query_local, build_local, scored_grads)


def on_device(feat_parts, dp_parts, query_grads, build_grads, scored_grads):
    feature_count = query_grads.shape[1]
    q_local, b_local = exchange(query_grads, build_grads, feat_parts, dp_parts)
    build_count, query_count = b_local.shape[0], q_local.shape[0]
    count, width = build_count // BLOCK, -(-query_count // BLOCK)
    used = count * (count + 1) // 2 + count * width + 1
    unit = max(1, feat_parts * dp_parts // 16)
    tile_count = -(-used // unit) * unit
    tiles = gram_tiles(q_local, b_local, tile_count)
    whole = sum_everywhere(tiles, feat_parts, dp_parts).reshape(tile_count, BLOCK, BLOCK)
    solved_half, scale = solve(whole, build_count, query_count, feature_count)
    return score(solved_half, scale, q_local, b_local, scored_grads, feat_parts, dp_parts)


def solution(mesh):
    placed = (P(("dp", "feat"), None), P("dp", "feat"), P("dp", "feat"))
    return jax.shard_map(
        functools.partial(on_device, mesh.shape["feat"], mesh.shape["dp"]),
        mesh=mesh,
        in_specs=placed,
        out_specs=P(("dp", "feat"), None),
        check_vma=False,
    )
```

```python
import functools

import jax
import jax.numpy as jnp
from jax import lax
from jax.experimental import pallas as pl
from jax.experimental.pallas import tpu as pltpu
from jax.sharding import PartitionSpec as P

BLOCK = 128
GROUP = 8
CHUNKS = 2


def contract_last(left, right):
    return lax.dot_general(
        left, right, (((1,), (1,)), ((), ())), preferred_element_type=jnp.float32
    )


def wide_dot(left, right, dims):
    return lax.dot_general(
        left,
        right,
        (dims, ((), ())),
        precision=lax.Precision.HIGHEST,
        preferred_element_type=jnp.float32,
    )


def invert_block(block):
    size = block.shape[0]
    lane = lax.broadcasted_iota(jnp.int32, (1, size), 1)
    row_id = lax.broadcasted_iota(jnp.int32, (GROUP, size), 0)
    inside = lane < GROUP

    def group(_, values):
        top, rest = values[:GROUP], values[GROUP:]
        columns = [jnp.broadcast_to(top[:, j : j + 1], (GROUP, size)) for j in range(GROUP)]
        for k in range(GROUP):
            at_k = row_id == k
            pivot = 1.0 / columns[k][k : k + 1]
            old = jnp.where(at_k, -1.0, columns[k]) * pivot
            for j in range(GROUP):
                if j != k:
                    columns[j] = jnp.where(at_k, 0.0, columns[j]) - old * columns[j][k : k + 1]
            columns[k] = -old
        rows = jnp.zeros((GROUP, size), jnp.float32)
        for j in range(GROUP):
            rows = rows + columns[j] * jnp.where(
                inside, jnp.where(lane == j, 1.0, 0.0), top[j : j + 1]
            )
        left = rest
        rest = jnp.where(inside, 0.0, rest)
        for j in range(GROUP):
            rest = rest - left[:, j : j + 1] * rows[j : j + 1]
        return pltpu.roll(jnp.concatenate([rest, rows], axis=0), size - GROUP, 1)

    return lax.fori_loop(0, size // GROUP, group, block, unroll=2)


def solve_kernel(count, feature_count, tiles_ref, half_ref, scale_ref, right, *strips):
    build_count = count * BLOCK
    width = right.shape[1] // BLOCK
    place = {}
    for i in range(count):
        for j in range(i, count):
            place[i, j] = len(place)
    eye = lax.broadcasted_iota(jnp.int32, (BLOCK, BLOCK), 0) == lax.broadcasted_iota(
        jnp.int32, (BLOCK, BLOCK), 1
    )
    diagonal = jnp.zeros((BLOCK, BLOCK), jnp.float32)
    for i in range(count):
        diagonal = diagonal + jnp.where(eye, tiles_ref[place[i, i]], 0.0)
    total = jnp.sum(jnp.sum(diagonal, axis=1, keepdims=True), axis=0, keepdims=True)
    damping = 0.1 * total / (build_count * feature_count) + 1e-06
    shift = jnp.where(eye, build_count * damping, 0.0)

    def lanes(i):
        return slice(i * BLOCK, (i + 1) * BLOCK)

    for i in range(count):
        for j in range(i, count):
            tile = tiles_ref[place[i, j]]
            strips[i][:, lanes(j - i)] = tile + shift if i == j else tile
        for j in range(width):
            strips[i][:, lanes(count - i + j)] = tiles_ref[len(place) + i * width + j]

    for k in range(count):
        inverse = invert_block(strips[k][:, :BLOCK])
        scaled = wide_dot(inverse, strips[k][:, BLOCK:], ((1,), (0,)))
        for i in range(k + 1, count):
            left = strips[k][:, lanes(i - k)]
            strips[i][...] -= wide_dot(left, scaled[:, (i - k - 1) * BLOCK :], ((0,), (0,)))
        strips[k][:, BLOCK:] = scaled
    for k in reversed(range(count)):
        end = (count - k) * BLOCK
        value = strips[k][:, end:]
        if k + 1 < count:
            value = value - wide_dot(
                strips[k][:, BLOCK:end], right[(k + 1) * BLOCK :, :], ((1,), (0,))
            )
        right[k * BLOCK : (k + 1) * BLOCK, :] = value
    half = right[...].astype(jnp.bfloat16)
    half_ref[...] = half
    last = len(place) + count * width
    for j in range(width):
        taken = jnp.zeros((1, BLOCK), jnp.float32)
        for i in range(count):
            block = half[lanes(i), lanes(j)].astype(jnp.float32)
            taken = taken + jnp.sum(
                block * tiles_ref[len(place) + i * width + j], axis=0, keepdims=True
            )
        kept = tiles_ref[last][j : j + 1, :] - taken
        scale_ref[:, lanes(j)] = 1.0 / jnp.sqrt(damping * kept)


def solve(tiles, build_count, query_count, feature_count):
    count = build_count // BLOCK
    wide = -(-query_count // BLOCK) * BLOCK
    vmem = pl.BlockSpec(memory_space=pltpu.VMEM)
    return pl.pallas_call(
        functools.partial(solve_kernel, count, feature_count),
        out_shape=(
            jax.ShapeDtypeStruct((build_count, wide), jnp.bfloat16),
            jax.ShapeDtypeStruct((1, wide), jnp.float32),
        ),
        in_specs=[vmem],
        out_specs=(vmem, vmem),
        scratch_shapes=[pltpu.VMEM((build_count, wide), jnp.float32)]
        + [pltpu.VMEM((BLOCK, (count - k) * BLOCK + wide), jnp.float32) for k in range(count)],
        compiler_params=pltpu.CompilerParams(vmem_limit_bytes=48 * 1024 * 1024),
    )(tiles)


MESH = pl.DeviceIdType.MESH


def exchange_kernel(
    feat_parts, dp_parts, query_ref, build_ref, query_out, build_out,
    local_sem, query_send, query_recv, build_send, build_recv,
):
    feat, dp = lax.axis_index("feat"), lax.axis_index("dp")
    parts = feat_parts * dp_parts
    me = dp * feat_parts + feat
    rows, span = build_ref.shape[0], build_out.shape[1]

    def peer(step):
        at = lax.rem(me + step, parts)
        return at, {"dp": at // feat_parts, "feat": lax.rem(at, feat_parts)}

    barrier = pltpu.get_barrier_semaphore()

    def greet(step, _):
        pl.semaphore_signal(barrier, inc=1, device_id=peer(step)[1], device_id_type=MESH)
        return 0

    lax.fori_loop(1, parts, greet, 0)
    pl.semaphore_wait(barrier, parts - 1)

    def query_copy(step):
        at, device = peer(step)
        return pltpu.make_async_remote_copy(
            src_ref=query_ref.at[at],
            dst_ref=query_out.at[me],
            send_sem=query_send.at[step],
            recv_sem=query_recv.at[step],
            device_id=device,
            device_id_type=MESH,
        )

    def columns(owner):
        return pl.ds(pl.multiple_of(owner * span, BLOCK), span)

    mine = pl.ds(pl.multiple_of(dp * rows, 16), rows)
    own = [
        pltpu.make_async_copy(build_ref.at[:, columns(dp)], build_out.at[mine], local_sem.at[0]),
        pltpu.make_async_copy(query_ref.at[me], query_out.at[me], local_sem.at[1]),
    ]
    sent = []
    for step in range(1, dp_parts):
        target = lax.rem(dp + step, dp_parts)
        sent.append(
            pltpu.make_async_remote_copy(
                src_ref=build_ref.at[:, columns(target)],
                dst_ref=build_out.at[mine],
                send_sem=build_send.at[step],
                recv_sem=build_recv.at[step],
                device_id={"dp": target, "feat": feat},
                device_id_type=MESH,
            )
        )

    def start_query(step, _):
        query_copy(step).start()
        return 0

    lax.fori_loop(1, parts, start_query, 0)
    for copy in sent + own:
        copy.start()

    def wait_query(step, _):
        query_copy(step).wait()
        return 0

    lax.fori_loop(1, parts, wait_query, 0)
    for copy in sent + own:
        copy.wait()


def exchange(query_grads, build_grads, feat_parts, dp_parts):
    parts = feat_parts * dp_parts
    rows, features = query_grads.shape
    span = features // parts
    arranged = query_grads.reshape(rows, feat_parts, dp_parts, span).transpose(2, 1, 0, 3)
    arranged = arranged.reshape(parts, rows * span // BLOCK, BLOCK)
    anywhere = pl.BlockSpec(memory_space=pl.ANY)
    query_out, build_out = pl.pallas_call(
        functools.partial(exchange_kernel, feat_parts, dp_parts),
        out_shape=(
            jax.ShapeDtypeStruct(arranged.shape, jnp.bfloat16),
            jax.ShapeDtypeStruct((build_grads.shape[0] * dp_parts, span), jnp.bfloat16),
        ),
        in_specs=[anywhere] * 2,
        out_specs=(anywhere, pl.BlockSpec(memory_space=pltpu.VMEM)),
        scratch_shapes=[
            pltpu.SemaphoreType.DMA((2,)),
            pltpu.SemaphoreType.DMA((parts,)),
            pltpu.SemaphoreType.DMA((parts,)),
            pltpu.SemaphoreType.DMA((dp_parts,)),
            pltpu.SemaphoreType.DMA((dp_parts,)),
        ],
        compiler_params=pltpu.CompilerParams(collective_id=0, has_side_effects=True),
    )(arranged, build_grads)
    return query_out.reshape(rows * parts, span), build_out


def gram_kernel(query_ref, build_ref, out_ref, gram, cross, square):
    build_count, features = build_ref.shape
    query_count = query_ref.shape[0]
    count = build_count // BLOCK
    step = min(512, features)
    strip = 2 * BLOCK if count % 2 == 0 else BLOCK
    gram[...] = jnp.zeros_like(gram)
    cross[...] = jnp.zeros_like(cross)
    square[...] = jnp.zeros_like(square)

    @pl.loop(0, features // step)
    def _(at):
        here = pl.ds(pl.multiple_of(at * step, BLOCK), step)
        build = build_ref[:, here]
        query = query_ref[:, here]
        for low in range(0, build_count, strip):
            gram[low : low + strip, low:] += contract_last(build[low : low + strip], build[low:])
        cross[:, :query_count] += contract_last(build, query)
        wide = query.astype(jnp.float32)
        square[...] += jnp.sum(wide * wide, axis=1, keepdims=True)

    place = 0
    for i in range(count):
        for j in range(i, count):
            out_ref[pl.ds(place * BLOCK, BLOCK), :] = gram[
                i * BLOCK : (i + 1) * BLOCK, j * BLOCK : (j + 1) * BLOCK
            ]
            place += 1
    width = cross.shape[1] // BLOCK
    for i in range(count):
        for j in range(width):
            out_ref[pl.ds(place * BLOCK, BLOCK), :] = cross[
                i * BLOCK : (i + 1) * BLOCK, j * BLOCK : (j + 1) * BLOCK
            ]
            place += 1
    out_ref[pl.ds(place * BLOCK, out_ref.shape[0] - place * BLOCK), :] = jnp.zeros(
        (out_ref.shape[0] - place * BLOCK, BLOCK), jnp.float32
    )
    for j in range(-(-query_count // BLOCK)):
        size = min(BLOCK, query_count - j * BLOCK)
        eye = lax.broadcasted_iota(jnp.int32, (size, BLOCK), 0) == lax.broadcasted_iota(
            jnp.int32, (size, BLOCK), 1
        )
        column = square[j * BLOCK : j * BLOCK + size, :]
        row = jnp.sum(jnp.where(eye, column, 0.0), axis=0, keepdims=True)
        out_ref[pl.ds(place * BLOCK + j, 1), :] = row


def gram_tiles(query_local, build_local, tile_count):
    build_count, query_count = build_local.shape[0], query_local.shape[0]
    wide = -(-query_count // BLOCK) * BLOCK
    vmem = pl.BlockSpec(memory_space=pltpu.VMEM)
    return pl.pallas_call(
        gram_kernel,
        out_shape=jax.ShapeDtypeStruct((tile_count * BLOCK, BLOCK), jnp.float32),
        in_specs=[vmem] * 2,
        out_specs=vmem,
        scratch_shapes=[
            pltpu.VMEM((build_count, build_count), jnp.float32),
            pltpu.VMEM((build_count, wide), jnp.float32),
            pltpu.VMEM((query_count, 1), jnp.float32),
        ],
        compiler_params=pltpu.CompilerParams(vmem_limit_bytes=48 * 1024 * 1024),
    )(query_local, build_local)


def sum_kernel(
    feat_parts, dp_parts, values_ref, whole_ref,
    pair_in, pair_sum, chip_in, chip_sum, feat_in, send_sem, recv_sem,
):
    feat, dp = lax.axis_index("feat"), lax.axis_index("dp")
    chips = dp_parts // 2
    core, chip = lax.rem(dp, 2), dp // 2
    total = values_ref.shape[0] // CHUNKS
    half, quarter, piece = total // 2, total // dp_parts, total // (dp_parts * feat_parts)

    def part(start, size):
        return pl.ds(pl.multiple_of(start, 8), size)

    other = {"dp": chip * 2 + 1 - core, "feat": feat}

    def along_chips(step):
        at = lax.rem(chip + step, chips)
        return at, {"dp": at * 2 + core, "feat": feat}

    def along_feat(step):
        at = lax.rem(feat + step, feat_parts)
        return at, {"dp": dp, "feat": at}

    barrier = pltpu.get_barrier_semaphore()
    peers = [other]
    peers += [along_chips(step)[1] for step in range(1, chips)]
    peers += [along_feat(step)[1] for step in range(1, feat_parts)]
    for device in peers:
        pl.semaphore_signal(barrier, inc=1, device_id=device, device_id_type=MESH)
    pl.semaphore_wait(barrier, len(peers))

    used = [0]

    def send(source, target, device):
        copy = pltpu.make_async_remote_copy(
            src_ref=source,
            dst_ref=target,
            send_sem=send_sem.at[used[0]],
            recv_sem=recv_sem.at[used[0]],
            device_id=device,
            device_id_type=MESH,
        )
        used[0] += 1
        copy.start()
        return copy

    chunks = range(CHUNKS)
    base = [c * total + core * half + chip * quarter for c in chunks]
    pair, along, across, gather, back, last = {}, {}, {}, {}, {}, {}
    for c in chunks:
        outgoing = values_ref.at[part(c * total + (1 - core) * half, half)]
        pair[c] = send(outgoing, pair_in.at[c], other)
    for c in chunks:
        pair[c].wait()
        pair_sum[c] = values_ref[part(c * total + core * half, half), :] + pair_in[c]
        along[c] = []
        for step in range(1, chips):
            at, device = along_chips(step)
            source = pair_sum.at[c, part(at * quarter, quarter)]
            along[c].append(send(source, chip_in.at[c, step - 1], device))
    for c in chunks:
        value = pair_sum[c, part(chip * quarter, quarter), :]
        for step, copy in enumerate(along[c]):
            copy.wait()
            value = value + chip_in[c, step]
        chip_sum[c] = value
        across[c] = []
        for step in range(1, feat_parts):
            at, device = along_feat(step)
            source = chip_sum.at[c, part(at * piece, piece)]
            across[c].append(send(source, feat_in.at[c, step - 1], device))
    for c in chunks:
        value = chip_sum[c, part(feat * piece, piece), :]
        for step, copy in enumerate(across[c]):
            copy.wait()
            value = value + feat_in[c, step]
        mine = whole_ref.at[part(base[c] + feat * piece, piece)]
        mine[...] = value
        gather[c] = [send(mine, mine, along_feat(step)[1]) for step in range(1, feat_parts)]
    for c in chunks:
        for copy in gather[c]:
            copy.wait()
        mine = whole_ref.at[part(base[c], quarter)]
        back[c] = [send(mine, mine, along_chips(step)[1]) for step in range(1, chips)]
    for c in chunks:
        for copy in back[c]:
            copy.wait()
        mine = whole_ref.at[part(c * total + core * half, half)]
        last[c] = send(mine, mine, other)
    for c in chunks:
        last[c].wait()


def sum_everywhere(values, feat_parts, dp_parts):
    total = values.shape[0] // CHUNKS
    chips = dp_parts // 2
    quarter, piece = total // dp_parts, total // (dp_parts * feat_parts)
    copies = 2 * CHUNKS * (1 + (chips - 1) + (feat_parts - 1))
    vmem = pl.BlockSpec(memory_space=pltpu.VMEM)
    return pl.pallas_call(
        functools.partial(sum_kernel, feat_parts, dp_parts),
        out_shape=jax.ShapeDtypeStruct(values.shape, jnp.float32),
        in_specs=[vmem],
        out_specs=vmem,
        scratch_shapes=[
            pltpu.VMEM((CHUNKS, total // 2, BLOCK), jnp.float32),
            pltpu.VMEM((CHUNKS, total // 2, BLOCK), jnp.float32),
            pltpu.VMEM((CHUNKS, max(1, chips - 1), quarter, BLOCK), jnp.float32),
            pltpu.VMEM((CHUNKS, quarter, BLOCK), jnp.float32),
            pltpu.VMEM((CHUNKS, max(1, feat_parts - 1), piece, BLOCK), jnp.float32),
            pltpu.SemaphoreType.DMA((copies,)),
            pltpu.SemaphoreType.DMA((copies,)),
        ],
        compiler_params=pltpu.CompilerParams(
            collective_id=1, has_side_effects=True, vmem_limit_bytes=48 * 1024 * 1024
        ),
    )(values)


def score_kernel(
    feat_parts, dp_parts, half_ref, scale_ref, query_ref, build_ref, scored_ref, out_ref,
    normed, scored, total, packed, arrived,
    load_sem, pair_send, pair_recv, chip_send, chip_recv, pass_send, pass_recv, feat_send, feat_recv,
):
    feat, dp = lax.axis_index("feat"), lax.axis_index("dp")
    chips = dp_parts // 2
    core, chip = lax.rem(dp, 2), dp // 2
    query_count, span = query_ref.shape
    rows = scored_ref.shape[0]
    pieces = normed.shape[0] // dp_parts
    size = span // pieces
    other = {"dp": chip * 2 + 1 - core, "feat": feat}

    def along_chips(step):
        return {"dp": lax.rem(chip + step, chips) * 2 + core, "feat": feat}

    def from_chip(step):
        return lax.rem(chip + chips - step, chips) * 2

    def along_feat(step):
        at = lax.rem(feat + step, feat_parts)
        return at, {"dp": dp, "feat": at}

    loads = []
    owners = [dp, chip * 2 + 1 - core]
    for step in range(1, chips):
        owners += [from_chip(step) + core, from_chip(step) + 1 - core]
    for at, owner in enumerate(owners):
        columns = pl.ds(pl.multiple_of(owner * span, BLOCK), span)
        load = pltpu.make_async_copy(scored_ref.at[:, columns], scored.at[at], load_sem.at[at])
        load.start()
        loads.append(load)

    peers = [other] + [along_chips(step) for step in range(1, chips)]
    peers += [along_feat(step)[1] for step in range(1, feat_parts)]
    barrier = pltpu.get_barrier_semaphore()
    for device in peers:
        pl.semaphore_signal(barrier, inc=1, device_id=device, device_id_type=MESH)
    pl.semaphore_wait(barrier, len(peers))

    def send(slot, device, send_sem, recv_sem):
        return pltpu.make_async_remote_copy(
            src_ref=normed.at[slot],
            dst_ref=normed.at[slot],
            send_sem=send_sem,
            recv_sem=recv_sem,
            device_id=device,
            device_id_type=MESH,
        )

    half = half_ref[:, :query_count]
    scale_row = scale_ref[:, :query_count]
    eye = lax.broadcasted_iota(jnp.int32, (query_count, query_count), 0) == lax.broadcasted_iota(
        jnp.int32, (query_count, query_count), 1
    )
    scale = jnp.sum(jnp.where(eye, scale_row, 0.0), axis=1, keepdims=True)
    sent, pairs, chip_copies = [], [], {}
    for piece in range(pieces):
        here = slice(piece * size, (piece + 1) * size)
        removed = lax.dot_general(
            half, build_ref[:, here], (((0,), (0,)), ((), ())), preferred_element_type=jnp.float32
        )
        value = (query_ref[:, here].astype(jnp.float32) - removed) * scale
        normed[dp * pieces + piece] = value.astype(jnp.bfloat16)
        for step in range(1, chips):
            at = (step - 1) * pieces + piece
            copy = send(dp * pieces + piece, along_chips(step), chip_send.at[at], chip_recv.at[at])
            copy.start()
            chip_copies[step, piece] = copy
        copy = send(dp * pieces + piece, other, pair_send.at[piece], pair_recv.at[piece])
        copy.start()
        pairs.append(copy)

    total[...] = jnp.zeros_like(total)

    def multiply(at, piece):
        left = scored.at[at]
        right = normed.at[owners[at] * pieces + piece]

        @pl.loop(0, rows // BLOCK)
        def _(row):
            here = pl.ds(pl.multiple_of(row * BLOCK, BLOCK), BLOCK)
            total[here, :] += contract_last(
                left[here, piece * size : (piece + 1) * size], right[...]
            )

    loads[0].wait()
    for piece in range(pieces):
        multiply(0, piece)
    loads[1].wait()
    for piece in range(pieces):
        pairs[piece].wait_recv()
        multiply(1, piece)
    passed = []
    for step in range(1, chips):
        loads[2 * step].wait()
        loads[2 * step + 1].wait()
    for piece in range(pieces):
        for step in range(1, chips):
            at = (step - 1) * pieces + piece
            chip_copies[step, piece].wait_recv()
            copy = send(
                (from_chip(step) + core) * pieces + piece, other, pass_send.at[at], pass_recv.at[at]
            )
            copy.start()
            multiply(2 * step, piece)
            copy.wait_recv()
            multiply(2 * step + 1, piece)
            passed.append(copy)
    for copy in pairs + list(chip_copies.values()) + passed:
        copy.wait_send()

    share = rows // feat_parts
    fold = packed.shape[2] // query_count
    part = share // fold
    for owner in range(feat_parts):
        blocks = [
            total[owner * share + at * part : owner * share + (at + 1) * part, :]
            for at in range(fold)
        ]
        packed[owner] = blocks[0] if fold == 1 else jnp.concatenate(blocks, axis=1)
    copies = []
    for step in range(1, feat_parts):
        at, device = along_feat(step)
        copy = pltpu.make_async_remote_copy(
            src_ref=packed.at[at],
            dst_ref=arrived.at[step - 1],
            send_sem=feat_send.at[step],
            recv_sem=feat_recv.at[step],
            device_id=device,
            device_id_type=MESH,
        )
        copy.start()
        copies.append(copy)
    value = packed[feat]
    for step, copy in enumerate(copies):
        copy.wait()
        value = value + arrived[step]
    for at in range(fold):
        out_ref[at * part : (at + 1) * part, :] = value[
            :, at * query_count : (at + 1) * query_count
        ]


def score(solved_half, scale, query_local, build_local, scored_grads, feat_parts, dp_parts):
    query_count, span = query_local.shape
    rows = scored_grads.shape[0]
    pieces = 2 if span % (2 * BLOCK) == 0 else 1
    chips = dp_parts // 2
    share = rows // feat_parts
    fold = BLOCK // query_count if query_count < BLOCK and share % (8 * BLOCK // query_count) == 0 else 1
    vmem = pl.BlockSpec(memory_space=pltpu.VMEM)
    remote = max(1, (chips - 1) * pieces)
    dma = pltpu.SemaphoreType.DMA
    return pl.pallas_call(
        functools.partial(score_kernel, feat_parts, dp_parts),
        out_shape=jax.ShapeDtypeStruct((share, query_count), jnp.float32),
        in_specs=[vmem] * 4 + [pl.BlockSpec(memory_space=pl.ANY)],
        out_specs=vmem,
        scratch_shapes=[
            pltpu.VMEM((dp_parts * pieces, query_count, span // pieces), jnp.bfloat16),
            pltpu.VMEM((dp_parts, rows, span), jnp.bfloat16),
            pltpu.VMEM((rows, query_count), jnp.float32),
            pltpu.VMEM((feat_parts, share // fold, query_count * fold), jnp.float32),
            pltpu.VMEM((max(1, feat_parts - 1), share // fold, query_count * fold), jnp.float32),
            dma((dp_parts,)),
            dma((pieces,)),
            dma((pieces,)),
            dma((remote,)),
            dma((remote,)),
            dma((remote,)),
            dma((remote,)),
            dma((feat_parts,)),
            dma((feat_parts,)),
        ],
        compiler_params=pltpu.CompilerParams(
            collective_id=2, has_side_effects=True, vmem_limit_bytes=48 * 1024 * 1024
        ),
    )(solved_half, scale, query_local, build_local, scored_grads)


def on_device(feat_parts, dp_parts, query_grads, build_grads, scored_grads):
    feature_count = query_grads.shape[1]
    q_local, b_local = exchange(query_grads, build_grads, feat_parts, dp_parts)
    build_count, query_count = b_local.shape[0], q_local.shape[0]
    count, width = build_count // BLOCK, -(-query_count // BLOCK)
    used = count * (count + 1) // 2 + count * width + 1
    unit = max(1, feat_parts * dp_parts * CHUNKS // 16)
    tile_count = -(-used // unit) * unit
    tiles = gram_tiles(q_local, b_local, tile_count)
    whole = sum_everywhere(tiles, feat_parts, dp_parts).reshape(tile_count, BLOCK, BLOCK)
    solved_half, scale = solve(whole, build_count, query_count, feature_count)
    return score(solved_half, scale, q_local, b_local, scored_grads, feat_parts, dp_parts)


def solution(mesh):
    placed = (P(("dp", "feat"), None), P("dp", "feat"), P("dp", "feat"))
    return jax.shard_map(
        functools.partial(on_device, mesh.shape["feat"], mesh.shape["dp"]),
        mesh=mesh,
        in_specs=placed,
        out_specs=P(("dp", "feat"), None),
        check_vma=False,
    )
```

```python
import functools

import jax
import jax.numpy as jnp
from jax import lax
from jax.experimental import pallas as pl
from jax.experimental.pallas import tpu as pltpu
from jax.sharding import PartitionSpec as P

BLOCK = 128
GROUP = 8
CHUNKS = 2
PIECES = 4


def contract_last(left, right):
    return lax.dot_general(
        left, right, (((1,), (1,)), ((), ())), preferred_element_type=jnp.float32
    )


def wide_dot(left, right, dims):
    return lax.dot_general(
        left,
        right,
        (dims, ((), ())),
        precision=lax.Precision.HIGHEST,
        preferred_element_type=jnp.float32,
    )


def invert_block(block):
    size = block.shape[0]
    lane = lax.broadcasted_iota(jnp.int32, (1, size), 1)
    row_id = lax.broadcasted_iota(jnp.int32, (GROUP, size), 0)
    inside = lane < GROUP

    def group(_, values):
        top, rest = values[:GROUP], values[GROUP:]
        columns = [jnp.broadcast_to(top[:, j : j + 1], (GROUP, size)) for j in range(GROUP)]
        for k in range(GROUP):
            at_k = row_id == k
            pivot = 1.0 / columns[k][k : k + 1]
            old = jnp.where(at_k, -1.0, columns[k]) * pivot
            for j in range(GROUP):
                if j != k:
                    columns[j] = jnp.where(at_k, 0.0, columns[j]) - old * columns[j][k : k + 1]
            columns[k] = -old
        rows = jnp.zeros((GROUP, size), jnp.float32)
        for j in range(GROUP):
            rows = rows + columns[j] * jnp.where(
                inside, jnp.where(lane == j, 1.0, 0.0), top[j : j + 1]
            )
        left = rest
        rest = jnp.where(inside, 0.0, rest)
        for j in range(GROUP):
            rest = rest - left[:, j : j + 1] * rows[j : j + 1]
        return pltpu.roll(jnp.concatenate([rest, rows], axis=0), size - GROUP, 1)

    return lax.fori_loop(0, size // GROUP, group, block, unroll=2)


def solve_kernel(count, feature_count, tiles_ref, half_ref, scale_ref, right, *strips):
    build_count = count * BLOCK
    width = right.shape[1] // BLOCK
    place = {}
    for i in range(count):
        for j in range(i, count):
            place[i, j] = len(place)
    eye = lax.broadcasted_iota(jnp.int32, (BLOCK, BLOCK), 0) == lax.broadcasted_iota(
        jnp.int32, (BLOCK, BLOCK), 1
    )
    diagonal = jnp.zeros((BLOCK, BLOCK), jnp.float32)
    for i in range(count):
        diagonal = diagonal + jnp.where(eye, tiles_ref[place[i, i]], 0.0)
    total = jnp.sum(jnp.sum(diagonal, axis=1, keepdims=True), axis=0, keepdims=True)
    damping = 0.1 * total / (build_count * feature_count) + 1e-06
    shift = jnp.where(eye, build_count * damping, 0.0)

    def lanes(i):
        return slice(i * BLOCK, (i + 1) * BLOCK)

    for i in range(count):
        for j in range(i, count):
            tile = tiles_ref[place[i, j]]
            strips[i][:, lanes(j - i)] = tile + shift if i == j else tile
        for j in range(width):
            strips[i][:, lanes(count - i + j)] = tiles_ref[len(place) + i * width + j]

    for k in range(count):
        inverse = invert_block(strips[k][:, :BLOCK])
        scaled = wide_dot(inverse, strips[k][:, BLOCK:], ((1,), (0,)))
        for i in range(k + 1, count):
            left = strips[k][:, lanes(i - k)]
            strips[i][...] -= wide_dot(left, scaled[:, (i - k - 1) * BLOCK :], ((0,), (0,)))
        strips[k][:, BLOCK:] = scaled
    for k in reversed(range(count)):
        end = (count - k) * BLOCK
        value = strips[k][:, end:]
        if k + 1 < count:
            value = value - wide_dot(
                strips[k][:, BLOCK:end], right[(k + 1) * BLOCK :, :], ((1,), (0,))
            )
        right[k * BLOCK : (k + 1) * BLOCK, :] = value
    half = right[...].astype(jnp.bfloat16)
    half_ref[...] = half
    last = len(place) + count * width
    for j in range(width):
        taken = jnp.zeros((1, BLOCK), jnp.float32)
        for i in range(count):
            block = half[lanes(i), lanes(j)].astype(jnp.float32)
            taken = taken + jnp.sum(
                block * tiles_ref[len(place) + i * width + j], axis=0, keepdims=True
            )
        kept = tiles_ref[last][j : j + 1, :] - taken
        scale_ref[:, lanes(j)] = 1.0 / jnp.sqrt(damping * kept)


MESH = pl.DeviceIdType.MESH


def exchange_kernel(
    feat_parts, dp_parts, query_ref, build_ref, query_out, build_out,
    local_sem, query_send, query_recv, build_send, build_recv,
):
    feat, dp = lax.axis_index("feat"), lax.axis_index("dp")
    parts = feat_parts * dp_parts
    me = dp * feat_parts + feat
    rows, span = build_ref.shape[0], build_out.shape[1]

    def peer(step):
        at = lax.rem(me + step, parts)
        return at, {"dp": at // feat_parts, "feat": lax.rem(at, feat_parts)}

    barrier = pltpu.get_barrier_semaphore()

    def greet(step, _):
        pl.semaphore_signal(barrier, inc=1, device_id=peer(step)[1], device_id_type=MESH)
        return 0

    lax.fori_loop(1, parts, greet, 0)
    pl.semaphore_wait(barrier, parts - 1)

    def query_copy(step):
        at, device = peer(step)
        return pltpu.make_async_remote_copy(
            src_ref=query_ref.at[at],
            dst_ref=query_out.at[me],
            send_sem=query_send.at[step],
            recv_sem=query_recv.at[step],
            device_id=device,
            device_id_type=MESH,
        )

    def columns(owner):
        return pl.ds(pl.multiple_of(owner * span, BLOCK), span)

    mine = pl.ds(pl.multiple_of(dp * rows, 16), rows)
    own = [
        pltpu.make_async_copy(build_ref.at[:, columns(dp)], build_out.at[mine], local_sem.at[0]),
        pltpu.make_async_copy(query_ref.at[me], query_out.at[me], local_sem.at[1]),
    ]
    sent = []
    for step in range(1, dp_parts):
        target = lax.rem(dp + step, dp_parts)
        sent.append(
            pltpu.make_async_remote_copy(
                src_ref=build_ref.at[:, columns(target)],
                dst_ref=build_out.at[mine],
                send_sem=build_send.at[step],
                recv_sem=build_recv.at[step],
                device_id={"dp": target, "feat": feat},
                device_id_type=MESH,
            )
        )

    def start_query(step, _):
        query_copy(step).start()
        return 0

    lax.fori_loop(1, parts, start_query, 0)
    for copy in sent + own:
        copy.start()

    def wait_query(step, _):
        query_copy(step).wait()
        return 0

    lax.fori_loop(1, parts, wait_query, 0)
    for copy in sent + own:
        copy.wait()


def exchange(query_grads, build_grads, feat_parts, dp_parts):
    parts = feat_parts * dp_parts
    rows, features = query_grads.shape
    span = features // parts
    arranged = query_grads.reshape(rows, feat_parts, dp_parts, span).transpose(2, 1, 0, 3)
    arranged = arranged.reshape(parts, rows * span // BLOCK, BLOCK)
    anywhere = pl.BlockSpec(memory_space=pl.ANY)
    query_out, build_out = pl.pallas_call(
        functools.partial(exchange_kernel, feat_parts, dp_parts),
        out_shape=(
            jax.ShapeDtypeStruct(arranged.shape, jnp.bfloat16),
            jax.ShapeDtypeStruct((build_grads.shape[0] * dp_parts, span), jnp.bfloat16),
        ),
        in_specs=[anywhere] * 2,
        out_specs=(anywhere, pl.BlockSpec(memory_space=pltpu.VMEM)),
        scratch_shapes=[
            pltpu.SemaphoreType.DMA((2,)),
            pltpu.SemaphoreType.DMA((parts,)),
            pltpu.SemaphoreType.DMA((parts,)),
            pltpu.SemaphoreType.DMA((dp_parts,)),
            pltpu.SemaphoreType.DMA((dp_parts,)),
        ],
        compiler_params=pltpu.CompilerParams(collective_id=0, has_side_effects=True),
    )(arranged, build_grads)
    return query_out.reshape(rows * parts, span), build_out


def gram_kernel(query_ref, build_ref, out_ref, gram, cross, square):
    build_count, features = build_ref.shape
    query_count = query_ref.shape[0]
    count = build_count // BLOCK
    step = min(512, features)
    strip = 2 * BLOCK if count % 2 == 0 else BLOCK
    gram[...] = jnp.zeros_like(gram)
    cross[...] = jnp.zeros_like(cross)
    square[...] = jnp.zeros_like(square)

    @pl.loop(0, features // step)
    def _(at):
        here = pl.ds(pl.multiple_of(at * step, BLOCK), step)
        build = build_ref[:, here]
        query = query_ref[:, here]
        for low in range(0, build_count, strip):
            gram[low : low + strip, low:] += contract_last(build[low : low + strip], build[low:])
        cross[:, :query_count] += contract_last(build, query)
        wide = query.astype(jnp.float32)
        square[...] += jnp.sum(wide * wide, axis=1, keepdims=True)

    place = 0
    for i in range(count):
        for j in range(i, count):
            out_ref[pl.ds(place * BLOCK, BLOCK), :] = gram[
                i * BLOCK : (i + 1) * BLOCK, j * BLOCK : (j + 1) * BLOCK
            ]
            place += 1
    width = cross.shape[1] // BLOCK
    for i in range(count):
        for j in range(width):
            out_ref[pl.ds(place * BLOCK, BLOCK), :] = cross[
                i * BLOCK : (i + 1) * BLOCK, j * BLOCK : (j + 1) * BLOCK
            ]
            place += 1
    out_ref[pl.ds(place * BLOCK, out_ref.shape[0] - place * BLOCK), :] = jnp.zeros(
        (out_ref.shape[0] - place * BLOCK, BLOCK), jnp.float32
    )
    for j in range(-(-query_count // BLOCK)):
        size = min(BLOCK, query_count - j * BLOCK)
        eye = lax.broadcasted_iota(jnp.int32, (size, BLOCK), 0) == lax.broadcasted_iota(
            jnp.int32, (size, BLOCK), 1
        )
        column = square[j * BLOCK : j * BLOCK + size, :]
        row = jnp.sum(jnp.where(eye, column, 0.0), axis=0, keepdims=True)
        out_ref[pl.ds(place * BLOCK + j, 1), :] = row


def sum_kernel(
    feat_parts, dp_parts, values_ref, whole_ref,
    pair_in, pair_sum, chip_in, chip_sum, feat_in, send_sem, recv_sem,
):
    feat, dp = lax.axis_index("feat"), lax.axis_index("dp")
    chips = dp_parts // 2
    core, chip = lax.rem(dp, 2), dp // 2
    total = values_ref.shape[0] // CHUNKS
    half, quarter, piece = total // 2, total // dp_parts, total // (dp_parts * feat_parts)

    def part(start, size):
        return pl.ds(pl.multiple_of(start, 8), size)

    other = {"dp": chip * 2 + 1 - core, "feat": feat}

    def along_chips(step):
        at = lax.rem(chip + step, chips)
        return at, {"dp": at * 2 + core, "feat": feat}

    def along_feat(step):
        at = lax.rem(feat + step, feat_parts)
        return at, {"dp": dp, "feat": at}

    used = [0]

    def send(source, target, device):
        copy = pltpu.make_async_remote_copy(
            src_ref=source,
            dst_ref=target,
            send_sem=send_sem.at[used[0]],
            recv_sem=recv_sem.at[used[0]],
            device_id=device,
            device_id_type=MESH,
        )
        used[0] += 1
        copy.start()
        return copy

    chunks = range(CHUNKS)
    base = [c * total + core * half + chip * quarter for c in chunks]
    pair, along, across, gather, back, last = {}, {}, {}, {}, {}, {}
    for c in chunks:
        outgoing = values_ref.at[part(c * total + (1 - core) * half, half)]
        pair[c] = send(outgoing, pair_in.at[c], other)
    for c in chunks:
        pair[c].wait()
        pair_sum[c] = values_ref[part(c * total + core * half, half), :] + pair_in[c]
        along[c] = []
        for step in range(1, chips):
            at, device = along_chips(step)
            source = pair_sum.at[c, part(at * quarter, quarter)]
            along[c].append(send(source, chip_in.at[c, step - 1], device))
    for c in chunks:
        value = pair_sum[c, part(chip * quarter, quarter), :]
        for step, copy in enumerate(along[c]):
            copy.wait()
            value = value + chip_in[c, step]
        chip_sum[c] = value
        across[c] = []
        for step in range(1, feat_parts):
            at, device = along_feat(step)
            source = chip_sum.at[c, part(at * piece, piece)]
            across[c].append(send(source, feat_in.at[c, step - 1], device))
    for c in chunks:
        value = chip_sum[c, part(feat * piece, piece), :]
        for step, copy in enumerate(across[c]):
            copy.wait()
            value = value + feat_in[c, step]
        mine = whole_ref.at[part(base[c] + feat * piece, piece)]
        mine[...] = value
        gather[c] = [send(mine, mine, along_feat(step)[1]) for step in range(1, feat_parts)]
    for c in chunks:
        for copy in gather[c]:
            copy.wait()
        mine = whole_ref.at[part(base[c], quarter)]
        back[c] = [send(mine, mine, along_chips(step)[1]) for step in range(1, chips)]
    for c in chunks:
        for copy in back[c]:
            copy.wait()
        mine = whole_ref.at[part(c * total + core * half, half)]
        last[c] = send(mine, mine, other)
    for c in chunks:
        last[c].wait()


def score_kernel(
    feat_parts, dp_parts, owners, loads, half_ref, scale_ref, query_ref, build_ref, out_ref,
    normed, scored, total, packed, arrived,
    pair_send, pair_recv, chip_send, chip_recv, pass_send, pass_recv, feat_send, feat_recv,
):
    feat, dp = lax.axis_index("feat"), lax.axis_index("dp")
    chips = dp_parts // 2
    core, chip = lax.rem(dp, 2), dp // 2
    query_count, span = query_ref.shape
    rows = total.shape[0]
    pieces = normed.shape[0] // dp_parts
    size = span // pieces
    other = {"dp": chip * 2 + 1 - core, "feat": feat}

    def along_chips(step):
        return {"dp": lax.rem(chip + step, chips) * 2 + core, "feat": feat}

    def from_chip(step):
        return lax.rem(chip + chips - step, chips) * 2

    def along_feat(step):
        at = lax.rem(feat + step, feat_parts)
        return at, {"dp": dp, "feat": at}

    def send(slot, device, send_sem, recv_sem):
        return pltpu.make_async_remote_copy(
            src_ref=normed.at[slot],
            dst_ref=normed.at[slot],
            send_sem=send_sem,
            recv_sem=recv_sem,
            device_id=device,
            device_id_type=MESH,
        )

    half = half_ref[:, :query_count]
    scale_row = scale_ref[:, :query_count]
    eye = lax.broadcasted_iota(jnp.int32, (query_count, query_count), 0) == lax.broadcasted_iota(
        jnp.int32, (query_count, query_count), 1
    )
    scale = jnp.sum(jnp.where(eye, scale_row, 0.0), axis=1, keepdims=True)
    sent, pairs, chip_copies = [], [], {}
    for piece in range(pieces):
        here = slice(piece * size, (piece + 1) * size)
        removed = lax.dot_general(
            half, build_ref[:, here], (((0,), (0,)), ((), ())), preferred_element_type=jnp.float32
        )
        value = (query_ref[:, here].astype(jnp.float32) - removed) * scale
        normed[dp * pieces + piece] = value.astype(jnp.bfloat16)
        for step in range(1, chips):
            at = (step - 1) * pieces + piece
            copy = send(dp * pieces + piece, along_chips(step), chip_send.at[at], chip_recv.at[at])
            copy.start()
            chip_copies[step, piece] = copy
        copy = send(dp * pieces + piece, other, pair_send.at[piece], pair_recv.at[piece])
        copy.start()
        pairs.append(copy)

    total[...] = jnp.zeros_like(total)

    def multiply(at, piece):
        left = scored.at[at]
        right = normed.at[owners[at] * pieces + piece]

        @pl.loop(0, rows // BLOCK)
        def _(row):
            here = pl.ds(pl.multiple_of(row * BLOCK, BLOCK), BLOCK)
            total[here, :] += contract_last(
                left[here, piece * size : (piece + 1) * size], right[...]
            )

    loads[0].wait()
    for piece in range(pieces):
        multiply(0, piece)
    loads[1].wait()
    for piece in range(pieces):
        pairs[piece].wait_recv()
        multiply(1, piece)
    passed = []
    for step in range(1, chips):
        loads[2 * step].wait()
        loads[2 * step + 1].wait()
    for piece in range(pieces):
        for step in range(1, chips):
            at = (step - 1) * pieces + piece
            chip_copies[step, piece].wait_recv()
            copy = send(
                (from_chip(step) + core) * pieces + piece, other, pass_send.at[at], pass_recv.at[at]
            )
            copy.start()
            multiply(2 * step, piece)
            copy.wait_recv()
            multiply(2 * step + 1, piece)
            passed.append(copy)
    for copy in pairs + list(chip_copies.values()) + passed:
        copy.wait_send()

    share = rows // feat_parts
    fold = packed.shape[2] // query_count
    part = share // fold
    for owner in range(feat_parts):
        blocks = [
            total[owner * share + at * part : owner * share + (at + 1) * part, :]
            for at in range(fold)
        ]
        packed[owner] = blocks[0] if fold == 1 else jnp.concatenate(blocks, axis=1)
    copies = []
    for step in range(1, feat_parts):
        at, device = along_feat(step)
        copy = pltpu.make_async_remote_copy(
            src_ref=packed.at[at],
            dst_ref=arrived.at[step - 1],
            send_sem=feat_send.at[step],
            recv_sem=feat_recv.at[step],
            device_id=device,
            device_id_type=MESH,
        )
        copy.start()
        copies.append(copy)
    value = packed[feat]
    for step, copy in enumerate(copies):
        copy.wait()
        value = value + arrived[step]
    for at in range(fold):
        out_ref[at * part : (at + 1) * part, :] = value[
            :, at * query_count : (at + 1) * query_count
        ]


class Tiles:
    def __init__(self, ref):
        self.ref = ref

    def __getitem__(self, at):
        return self.ref[at * BLOCK : (at + 1) * BLOCK, :]


def main_kernel(
    feat_parts, dp_parts, feature_count, sizes, query_ref, build_ref, scored_ref, out_ref, *scratch
):
    scratch = list(scratch)
    groups = []
    for size in sizes:
        groups.append(scratch[:size])
        scratch = scratch[size:]
    (tiles, whole, half, scale, load_sem), for_gram, for_sum, for_solve, for_score = groups
    scored = for_score[1]
    feat, dp = lax.axis_index("feat"), lax.axis_index("dp")
    chips = dp_parts // 2
    core, chip = lax.rem(dp, 2), dp // 2
    span = query_ref.shape[1]

    peers = [{"dp": chip * 2 + 1 - core, "feat": feat}]
    owners = [dp, chip * 2 + 1 - core]
    for step in range(1, chips):
        peers.append({"dp": lax.rem(chip + step, chips) * 2 + core, "feat": feat})
        sender = lax.rem(chip + chips - step, chips) * 2
        owners += [sender + core, sender + 1 - core]
    for step in range(1, feat_parts):
        peers.append({"dp": dp, "feat": lax.rem(feat + step, feat_parts)})
    barrier = pltpu.get_barrier_semaphore()
    for device in peers:
        pl.semaphore_signal(barrier, inc=1, device_id=device, device_id_type=MESH)

    loads = []
    for at, owner in enumerate(owners):
        columns = pl.ds(pl.multiple_of(owner * span, BLOCK), span)
        load = pltpu.make_async_copy(scored_ref.at[:, columns], scored.at[at], load_sem.at[at])
        load.start()
        loads.append(load)

    gram_kernel(query_ref, build_ref, tiles, *for_gram)
    pl.semaphore_wait(barrier, len(peers))
    sum_kernel(feat_parts, dp_parts, tiles, whole, *for_sum)
    count = build_ref.shape[0] // BLOCK
    solve_kernel(count, feature_count, Tiles(whole), half, scale, *for_solve)
    score_kernel(
        feat_parts, dp_parts, owners, loads, half, scale, query_ref, build_ref, out_ref, *for_score
    )


def influence(query_local, build_local, scored_grads, feature_count, feat_parts, dp_parts):
    query_count, span = query_local.shape
    build_count = build_local.shape[0]
    rows = scored_grads.shape[0]
    count, width = build_count // BLOCK, -(-query_count // BLOCK)
    wide = width * BLOCK
    used = count * (count + 1) // 2 + count * width + 1
    unit = max(1, feat_parts * dp_parts * CHUNKS // 16)
    flat = -(-used // unit) * unit * BLOCK
    chips = dp_parts // 2
    chunk = flat // CHUNKS
    quarter, piece = chunk // dp_parts, chunk // (dp_parts * feat_parts)
    copies = 2 * CHUNKS * (1 + (chips - 1) + (feat_parts - 1))
    pieces = PIECES if span % (PIECES * BLOCK) == 0 else 1
    share = rows // feat_parts
    fold = BLOCK // query_count if query_count < BLOCK and share % (8 * BLOCK // query_count) == 0 else 1
    remote = max(1, (chips - 1) * pieces)
    vmem, dma = pltpu.VMEM, pltpu.SemaphoreType.DMA
    shared = [
        vmem((flat, BLOCK), jnp.float32),
        vmem((flat, BLOCK), jnp.float32),
        vmem((build_count, wide), jnp.bfloat16),
        vmem((1, wide), jnp.float32),
        dma((dp_parts,)),
    ]
    for_gram = [
        vmem((build_count, build_count), jnp.float32),
        vmem((build_count, wide), jnp.float32),
        vmem((query_count, 1), jnp.float32),
    ]
    for_sum = [
        vmem((CHUNKS, chunk // 2, BLOCK), jnp.float32),
        vmem((CHUNKS, chunk // 2, BLOCK), jnp.float32),
        vmem((CHUNKS, max(1, chips - 1), quarter, BLOCK), jnp.float32),
        vmem((CHUNKS, quarter, BLOCK), jnp.float32),
        vmem((CHUNKS, max(1, feat_parts - 1), piece, BLOCK), jnp.float32),
        dma((copies,)),
        dma((copies,)),
    ]
    for_solve = [vmem((build_count, wide), jnp.float32)]
    for_solve += [vmem((BLOCK, (count - k) * BLOCK + wide), jnp.float32) for k in range(count)]
    for_score = [
        vmem((dp_parts * pieces, query_count, span // pieces), jnp.bfloat16),
        vmem((dp_parts, rows, span), jnp.bfloat16),
        vmem((rows, query_count), jnp.float32),
        vmem((feat_parts, share // fold, query_count * fold), jnp.float32),
        vmem((max(1, feat_parts - 1), share // fold, query_count * fold), jnp.float32),
        dma((pieces,)),
        dma((pieces,)),
        dma((remote,)),
        dma((remote,)),
        dma((remote,)),
        dma((remote,)),
        dma((feat_parts,)),
        dma((feat_parts,)),
    ]
    groups = [shared, for_gram, for_sum, for_solve, for_score]
    sizes = [len(group) for group in groups]
    inside = pl.BlockSpec(memory_space=pltpu.VMEM)
    return pl.pallas_call(
        functools.partial(main_kernel, feat_parts, dp_parts, feature_count, sizes),
        out_shape=jax.ShapeDtypeStruct((share, query_count), jnp.float32),
        in_specs=[inside, inside, pl.BlockSpec(memory_space=pl.ANY)],
        out_specs=inside,
        scratch_shapes=sum(groups, []),
        compiler_params=pltpu.CompilerParams(
            collective_id=1, has_side_effects=True, vmem_limit_bytes=52 * 1024 * 1024
        ),
    )(query_local, build_local, scored_grads)


def on_device(feat_parts, dp_parts, query_grads, build_grads, scored_grads):
    q_local, b_local = exchange(query_grads, build_grads, feat_parts, dp_parts)
    feature_count = query_grads.shape[1]
    return influence(q_local, b_local, scored_grads, feature_count, feat_parts, dp_parts)


def solution(mesh):
    placed = (P(("dp", "feat"), None), P("dp", "feat"), P("dp", "feat"))
    return jax.shard_map(
        functools.partial(on_device, mesh.shape["feat"], mesh.shape["dp"]),
        mesh=mesh,
        in_specs=placed,
        out_specs=P(("dp", "feat"), None),
        check_vma=False,
    )
```
